512 devices in a mesh: section: 64 (over y_lo, z, core), uly: 8 (over x, y_hi).
Axes of the slice: x: 4, y: 8 (y_hi: 2, y_lo: 4; y = y_hi * 4 + y_lo), z: 8, core: 2. Of those that a mesh axis runs over, the one named last changes fastest.
Arguments:
- block_in: bfloat16 [64, 64, 2048], P('section', 'uly'), may hold values from -6 to 6
- fresh_patches: bfloat16 [3, 64, 2048], P(None, 'uly'), may hold values from -6 to 6
- w_qkv: bfloat16 [64, 2048, 3, 2048], P('section', None, None, 'uly'), may hold values from -0.125 to 0.125
- mod_shift: float32 [64, 2048], P('section'), may hold values from -3 to 3
- mod_scale: float32 [64, 2048], P('section'), may hold values from -0.5 to 0.5
- gate: float32 [64, 2048], P('section'), may hold values from 1 to 3
- q_gain: float32 [64, 128], P('section'), may hold values from 0.5 to 1.5
- k_gain: float32 [64, 128], P('section'), may hold values from 0.5 to 1.5
- image_cache: bfloat16 [64, 2, 512, 2048], P('section', None, None, 'uly'), may hold values from -6 to 6
- text_cache: bfloat16 [64, 2, 128, 2048], P('section', None, None, 'uly'), may hold values from -6 to 6
- patch_order: int32 [8], replicated, may hold values from 0 to 7, each once
- text_length: int32 [1], replicated, may hold values from 64 to 128
Outputs:
- block_out: bfloat16 [64, 64, 2048], P('section', 'uly')
- cache_out: bfloat16 [64, 2, 512, 2048], P('section', None, None, 'uly')
The draws below stay inside these ranges and needn't reach their ends.
All inputs are finite; a program needn't handle non-finite values.
Results may differ from the reference program's by a relative error of at most 0.0095.
Values may be sent and summed in bfloat16 or wider, within the bound.
A program may use at most 64 MiB of HBM per device.

```python
import math
import jax
import jax.numpy as jnp
from jax import lax

HEADS = 16
HD = 128
D = 2048
PR = 64
PATCHES = 8
TXT_MAX = 128
TICKS = 4
IMG = 512
SECTIONS = 64
N_SECTION = 64


def shard_levels(rng, extent, shards, least, top_value):
    factor_of, own = 1.0, jax.random.fold_in(rng, 6)
    for dim, parts in shards:
        steps = jnp.exp(jax.random.uniform(jax.random.fold_in(own, dim), (parts,), jnp.float32, least / len(shards), top_value / len(shards)))
        factor_of = factor_of * jnp.repeat(steps, extent[dim] // parts).reshape([-1 if axis == dim else 1 for axis in range(len(extent))])
    return factor_of


def normal_values(own_key, extent, spread, limit, cuts=(), held_as=jnp.bfloat16):
    array = jax.random.normal(own_key, extent, jnp.float32) * spread
    if len(cuts) > 0:
        array = shard_levels(own_key, extent, cuts, -0.22, 0.18) * array
    return jnp.clip(array, min=-limit, max=limit).astype(held_as)


def setup_inputs(seed: int = 0) -> dict:
    splits = jax.random.split(jax.random.key(seed), 13)
    return {
        "block_in": normal_values(splits[0], (SECTIONS, PR, D), 1.0, 6.0, ((0, 64), (1, 8))),
        "fresh_patches": normal_values(splits[1], (TICKS - 1, PR, D), 1.0, 6.0, ((1, 8),)),
        "w_qkv": normal_values(splits[2], (SECTIONS, D, 3, D), D ** -0.5, 0.125, ((0, 64), (3, 8))),
        "mod_shift": normal_values(splits[3], (SECTIONS, D), 0.5, 3.0, ((0, 64),), jnp.float32),
        "mod_scale": jnp.clip(jax.random.uniform(splits[4], (SECTIONS, D), jnp.float32, -0.5, 0.5) * shard_levels(splits[4], (SECTIONS, D), ((0, 64),), -0.4, 0.0), -0.5, 0.5),
        "gate": jnp.clip(1.0 + 2.0 * jax.random.uniform(splits[5], (SECTIONS, D), jnp.float32) ** shard_levels(splits[5], (SECTIONS, D), ((0, 64),), -0.2, 0.2), 1.0, 3.0),
        "q_gain": jnp.clip(1.0 + 0.1 * jax.random.normal(splits[6], (SECTIONS, HD), jnp.float32), 0.5, 1.5),
        "k_gain": jnp.clip(1.0 + 0.1 * jax.random.normal(splits[7], (SECTIONS, HD), jnp.float32), 0.5, 1.5),
        "image_cache": normal_values(splits[8], (SECTIONS, 2, IMG, D), 1.0, 6.0, ((0, 64), (3, 8))),
        "text_cache": normal_values(splits[9], (SECTIONS, 2, TXT_MAX, D), 1.0, 6.0, ((0, 64), (3, 8))),
        "patch_order": jax.random.permutation(splits[10], PATCHES).astype(jnp.int32),
        "text_length": jax.random.randint(splits[11], (1,), TXT_MAX // 2, TXT_MAX + 1).astype(jnp.int32),
    }


def head_norm(values, gain):
    factor = lax.rsqrt(lax.optimization_barrier(jnp.mean(values * values, axis=-1, keepdims=True)) + 1e-06)
    return values * factor * gain

def reference(block_in, fresh_patches, w_qkv, mod_shift, mod_scale, gate, q_gain, k_gain, image_cache, text_cache, patch_order, text_length):
    valid = (jnp.arange(TXT_MAX) < text_length[0]).astype(jnp.float32)
    mask = jnp.concatenate([valid, jnp.ones((IMG,), jnp.float32)])
    section_ids = jnp.arange(N_SECTION, dtype=jnp.int32)

    def run_tick(tick, stream, caches):

        def one_section(items):
            stream_row, weights, shift_row, scale_row, gate_row, q_row, k_row, cache, text, section_id = items
            xf = stream_row.astype(jnp.float32)
            centered = xf - lax.optimization_barrier(jnp.mean(xf, axis=-1, keepdims=True))
            variance = lax.optimization_barrier(jnp.mean(centered * centered, axis=-1, keepdims=True))
            modulated = (centered * lax.rsqrt(variance + 1e-06) * (1.0 + scale_row) + shift_row).astype(jnp.bfloat16)
            projected = jnp.dot(modulated, weights.reshape(D, 3 * D), preferred_element_type=jnp.float32)
            queries = head_norm(projected[:, :D].reshape(PR, HEADS, HD), q_row).astype(jnp.bfloat16)
            new_keys = projected[:, D:2 * D].astype(jnp.bfloat16)
            new_values = projected[:, 2 * D:].astype(jnp.bfloat16)
            slot = jnp.mod(tick - section_id, PATCHES).astype(jnp.int32)
            start = (patch_order[slot] * PR).astype(jnp.int32)
            cache = lax.dynamic_update_slice(cache, jnp.stack([new_keys, new_values]), (jnp.int32(0), start, jnp.int32(0)))
            keys_all = jnp.concatenate([text[0], cache[0]], axis=0).astype(jnp.float32).reshape(-1, HEADS, HD)
            keys_all = head_norm(keys_all, k_row).astype(jnp.bfloat16)
            values_all = jnp.concatenate([text[1], cache[1]], axis=0).reshape(-1, HEADS, HD)
            scores = jnp.einsum('rhd,khd->hrk', queries.astype(jnp.float32), keys_all.astype(jnp.float32)) / math.sqrt(HD)
            terms = jnp.exp(scores) * mask
            weight = (terms / lax.optimization_barrier(jnp.sum(terms, axis=-1, keepdims=True))).astype(jnp.bfloat16)
            attended = jnp.einsum('hrk,khd->rhd', weight.astype(jnp.float32), values_all.astype(jnp.float32))
            attended = attended.astype(jnp.bfloat16).reshape(PR, D)
            result = (xf + gate_row * attended.astype(jnp.float32)).astype(jnp.bfloat16)
            return (result, cache)
        return lax.map(one_section, (stream, w_qkv, mod_shift, mod_scale, gate, q_gain, k_gain, caches, text_cache, section_ids))
    stream = block_in
    caches = image_cache
    result = block_in
    for tick in range(TICKS):
        result, caches = run_tick(tick, stream, caches)
        if tick + 1 < TICKS:
            stream = jnp.concatenate([fresh_patches[tick][None], result[:-1]], axis=0)
    return (result, caches)
```

```python
import functools
import math

import jax
import jax.numpy as jnp
from jax import lax
from jax.experimental import pallas as pl
from jax.experimental.pallas import tpu as pltpu
from jax.sharding import PartitionSpec as P

MESH = pl.DeviceIdType.MESH
F32 = jnp.float32
BF16 = jnp.bfloat16
EPS = 1e-06


def head_factor(values):
    return lax.rsqrt(jnp.mean(values * values, axis=-1, keepdims=True) + EPS)


def normed(values, gain, head_dim):
    parts = []
    for start in range(0, values.shape[1], head_dim):
        part = values[:, start : start + head_dim]
        parts.append(part * head_factor(part) * gain)
    return jnp.concatenate(parts, axis=1)


def kernel(
    dims,
    block_hbm,
    fresh_hbm,
    w_hbm,
    shift_hbm,
    scale_hbm,
    gate_hbm,
    q_gain_hbm,
    k_gain_hbm,
    image_hbm,
    text_hbm,
    order_ref,
    length_ref,
    out_ref,
    cache_out_hbm,
    block,
    fresh,
    w,
    shift,
    scale,
    gate,
    q_gain,
    k_gain,
    raw,
    text,
    keys,
    values,
    stream,
    mod,
    sent,
    row_send,
    row_recv,
    last_send,
    last_recv,
    cache_stage,
    load_sem,
    store_sem,
    row_send_sem,
    row_recv_sem,
    tick_send_sem,
    tick_recv_sem,
    last_send_sem,
    last_recv_sem,
):
    sections, group, ticks, patches, pr, width, local, hd, txt = dims
    heads = local // hd
    img = patches * pr
    rows_dev = pr // group
    half = width // 2
    section = lax.axis_index("section")
    uly = lax.axis_index("uly")

    def peer(k):
        return lax.rem(uly + k, group)

    barrier = pltpu.get_barrier_semaphore()
    for k in range(1, group):
        pl.semaphore_signal(barrier, inc=1, device_id=(section, peer(k)), device_id_type=MESH)

    @pl.when(section > 0)
    def _():
        for k in range(group):
            pl.semaphore_signal(barrier, inc=1, device_id=(section - 1, peer(k)), device_id_type=MESH)

    loads = [
        pltpu.make_async_copy(src, dst, load_sem.at[i])
        for i, (src, dst) in enumerate(
            [
                (block_hbm, block),
                (fresh_hbm, fresh),
                (text_hbm, text),
                (k_gain_hbm, k_gain),
                (image_hbm, raw.at[:, pl.ds(0, img), :]),
                (shift_hbm, shift),
                (scale_hbm, scale),
                (gate_hbm, gate),
                (q_gain_hbm, q_gain),
                (w_hbm, w),
            ]
        )
    ]
    for copy in loads:
        copy.start()

    loads[0].wait()
    loads[1].wait()
    own = block[...].astype(F32)
    row_send[0] = jnp.concatenate([own[:, :half], own[:, half:]], axis=0).astype(BF16)
    for t in range(1, ticks):
        own = fresh[t - 1].astype(F32)
        row_send[t] = jnp.concatenate([own[:, :half], own[:, half:]], axis=0).astype(BF16)

    pl.semaphore_wait(barrier, group - 1 + jnp.where(section < sections - 1, group, 0))

    def row_copy(t, k):
        return pltpu.make_async_remote_copy(
            src_ref=row_send.at[t],
            dst_ref=row_recv.at[t, uly],
            send_sem=row_send_sem.at[t, k],
            recv_sem=row_recv_sem.at[t, uly],
            device_id=(section, peer(k)),
            device_id_type=MESH,
        )

    def row_arrival(t, k):
        return pltpu.make_async_remote_copy(
            src_ref=row_send.at[t],
            dst_ref=row_recv.at[t, peer(k)],
            send_sem=row_send_sem.at[t, k],
            recv_sem=row_recv_sem.at[t, peer(k)],
            device_id=(section, peer(k)),
            device_id_type=MESH,
        )

    for k in range(1, group):
        row_copy(0, k).start()

    @pl.when(section == 0)
    def _():
        for t in range(1, ticks):
            for k in range(1, group):
                row_copy(t, k).start()

    row_recv[0, uly] = row_send[0]
    for t in range(1, ticks):
        row_recv[t, uly] = row_send[t]

    def patch_at(slot):
        return order_ref[lax.rem(slot - section + sections * patches, patches)]

    loads[2].wait()
    loads[3].wait()
    loads[4].wait()
    k_row = k_gain[...]
    keys[pl.ds(0, txt), :] = normed(text[0].astype(F32), k_row, hd).astype(BF16)
    values[pl.ds(0, txt), :] = text[1]
    for j in range(patches):
        patch = patch_at(j)
        met = []
        for i in range(2):
            rows = raw[i, pl.ds(0, pr), :]
            for b in range(1, patches):
                rows = jnp.where(patch == b, raw[i, pl.ds(b * pr, pr), :], rows)
            met.append(rows)
        keys[pl.ds(txt + j * pr, pr), :] = normed(met[0].astype(F32), k_row, hd).astype(BF16)
        values[pl.ds(txt + j * pr, pr), :] = met[1]
    for copy in loads[5:]:
        copy.wait()
    q_row = q_gain[...]
    valid = (
        lax.broadcasted_iota(jnp.int32, (1, txt), 1) < length_ref[0]
    ).astype(F32)

    def rows_to_stream(t):
        for k in range(1, group):
            row_arrival(t, k).wait_recv()
        pieces = [row_recv[t, i].astype(F32) for i in range(group)]
        for side in range(2):
            whole = jnp.concatenate(
                [piece[side * rows_dev : (side + 1) * rows_dev] for piece in pieces], axis=0
            ).astype(BF16)
            for c in range(group // 2):
                stream[t, side * (group // 2) + c] = whole[:, c * local : (c + 1) * local]

    def tick_copy(t, k):
        return pltpu.make_async_remote_copy(
            src_ref=sent.at[t],
            dst_ref=stream.at[t + 1, uly],
            send_sem=tick_send_sem.at[t, k],
            recv_sem=tick_recv_sem.at[t + 1, uly],
            device_id=(section + 1, peer(k)),
            device_id_type=MESH,
        )

    def tick_arrival(t, k):
        return pltpu.make_async_remote_copy(
            src_ref=sent.at[t],
            dst_ref=stream.at[t, k],
            send_sem=tick_send_sem.at[t, k],
            recv_sem=tick_recv_sem.at[t, k],
            device_id=(section, uly),
            device_id_type=MESH,
        )

    def last_copy(k):
        return pltpu.make_async_remote_copy(
            src_ref=last_send.at[peer(k)],
            dst_ref=last_recv.at[uly],
            send_sem=last_send_sem.at[k],
            recv_sem=last_recv_sem.at[uly],
            device_id=(section, peer(k)),
            device_id_type=MESH,
        )

    def last_arrival(k):
        return pltpu.make_async_remote_copy(
            src_ref=last_send.at[peer(k)],
            dst_ref=last_recv.at[peer(k)],
            send_sem=last_send_sem.at[k],
            recv_sem=last_recv_sem.at[peer(k)],
            device_id=(section, peer(k)),
            device_id_type=MESH,
        )

    for t in range(ticks):
        if t == 0:
            rows_to_stream(0)
        else:

            @pl.when(section == 0)
            def _():
                rows_to_stream(t)

            @pl.when(section > 0)
            def _():
                for k in range(group):
                    tick_arrival(t, k).wait_recv()

        chunks = [stream[t, c].astype(F32) for c in range(group)]
        mean = jnp.sum(sum(chunks), axis=-1, keepdims=True) / width
        centered = [chunk - mean for chunk in chunks]
        variance = jnp.sum(sum(c * c for c in centered), axis=-1, keepdims=True) / width
        factor = lax.rsqrt(variance + EPS)
        for c in range(group):
            at = pl.ds(c * local, local)
            mod[:, at] = (centered[c] * factor * (1.0 + scale[:, at]) + shift[:, at]).astype(BF16)
        queries, new_keys, new_values = [
            jnp.dot(mod[...], w[j], preferred_element_type=F32) for j in range(3)
        ]
        queries = normed(queries, q_row, hd).astype(BF16)
        new_keys = new_keys.astype(BF16)
        new_values = new_values.astype(BF16)
        raw[0, pl.ds(img + t * pr, pr), :] = new_keys
        raw[1, pl.ds(img + t * pr, pr), :] = new_values
        keys[pl.ds(txt + t * pr, pr), :] = normed(new_keys.astype(F32), k_row, hd).astype(BF16)
        values[pl.ds(txt + t * pr, pr), :] = new_values

        if t == ticks - 1:
            for b in range(patches):
                for i in range(2):
                    rows = raw[i, pl.ds(b * pr, pr), :]
                    for j in range(ticks):
                        rows = jnp.where(
                            patch_at(j) == b, raw[i, pl.ds(img + j * pr, pr), :], rows
                        )
                    cache_stage[i, pl.ds(b * pr, pr), :] = rows
            store = pltpu.make_async_copy(cache_stage, cache_out_hbm, store_sem)
            store.start()

        results = []
        for h in range(heads):
            at = slice(h * hd, (h + 1) * hd)
            score = lax.dot_general(
                queries[:, at],
                keys[:, at],
                (((1,), (1,)), ((), ())),
                preferred_element_type=F32,
            )
            term = jnp.exp(score * (1.0 / math.sqrt(hd)))
            term = jnp.concatenate([term[:, :txt] * valid, term[:, txt:]], axis=1)
            total = jnp.sum(term, axis=-1, keepdims=True)
            weight = (term / total).astype(BF16)
            results.append(jnp.dot(weight, values[:, at], preferred_element_type=F32))
        attended = jnp.concatenate(results, axis=1).astype(BF16).astype(F32)
        own_at = pl.ds(pl.multiple_of(uly * local, local), local)
        result = stream[t, uly].astype(F32) + gate[:, own_at] * attended

        if t < ticks - 1:
            sent[t] = result.astype(BF16)

            @pl.when(section < sections - 1)
            def _():
                for k in range(group):
                    tick_copy(t, k).start()
        else:
            for i in range(group):
                piece = result[i * rows_dev : (i + 1) * rows_dev]
                last_send[i] = jnp.concatenate(
                    [piece[:, c * hd : (c + 1) * hd] for c in range(heads)], axis=0
                ).astype(BF16)
            for k in range(1, group):
                last_copy(k).start()
            last_recv[uly] = last_send[uly]

    for k in range(1, group):
        row_copy(0, k).wait_send()

    @pl.when(section == 0)
    def _():
        for t in range(1, ticks):
            for k in range(1, group):
                row_copy(t, k).wait_send()

    @pl.when(section < sections - 1)
    def _():
        for t in range(ticks - 1):
            for k in range(group):
                tick_copy(t, k).wait_send()

    for k in range(1, group):
        last_arrival(k).wait_recv()
    for i in range(group):
        piece = last_recv[i].astype(F32)
        for c in range(heads):
            out_ref[:, pl.ds(i * local + c * hd, hd)] = piece[
                c * rows_dev : (c + 1) * rows_dev
            ].astype(BF16)
    for k in range(1, group):
        last_copy(k).wait_send()
    store.wait()


def body(
    block_in,
    fresh_patches,
    w_qkv,
    mod_shift,
    mod_scale,
    gate,
    q_gain,
    k_gain,
    image_cache,
    text_cache,
    patch_order,
    text_length,
):
    sections, group = lax.axis_size("section"), lax.axis_size("uly")
    rows_dev, width = block_in.shape[1:]
    local = w_qkv.shape[3]
    hd = q_gain.shape[1]
    patches = patch_order.shape[0]
    ticks = fresh_patches.shape[0] + 1
    pr = rows_dev * group
    txt = text_cache.shape[2]
    img = patches * pr
    heads = local // hd
    dims = (sections, group, ticks, patches, pr, width, local, hd, txt)
    hbm = pl.BlockSpec(memory_space=pltpu.HBM)
    smem = pl.BlockSpec(memory_space=pltpu.SMEM)
    dma = pltpu.SemaphoreType.DMA
    out, cache = pl.pallas_call(
        functools.partial(kernel, dims),
        out_shape=(
            jax.ShapeDtypeStruct((rows_dev, width), BF16),
            jax.ShapeDtypeStruct((2, img, local), BF16),
        ),
        in_specs=[hbm] * 10 + [smem] * 2,
        out_specs=(pl.BlockSpec(memory_space=pltpu.VMEM), hbm),
        scratch_shapes=[
            pltpu.VMEM((rows_dev, width), BF16),
            pltpu.VMEM((ticks - 1, rows_dev, width), BF16),
            pltpu.VMEM((3, width, local), BF16),
            pltpu.VMEM((1, width), F32),
            pltpu.VMEM((1, width), F32),
            pltpu.VMEM((1, width), F32),
            pltpu.VMEM((1, hd), F32),
            pltpu.VMEM((1, hd), F32),
            pltpu.VMEM((2, img + ticks * pr, local), BF16),
            pltpu.VMEM((2, txt, local), BF16),
            pltpu.VMEM((txt + img, local), BF16),
            pltpu.VMEM((txt + img, local), BF16),
            pltpu.VMEM((ticks, group, pr, local), BF16),
            pltpu.VMEM((pr, width), BF16),
            pltpu.VMEM((ticks, pr, local), BF16),
            pltpu.VMEM((ticks, 2 * rows_dev, width // 2), BF16),
            pltpu.VMEM((ticks, group, 2 * rows_dev, width // 2), BF16),
            pltpu.VMEM((group, heads * rows_dev, hd), BF16),
            pltpu.VMEM((group, heads * rows_dev, hd), BF16),
            pltpu.VMEM((2, img, local), BF16),
            dma((10,)),
            dma,
            dma((ticks, group)),
            dma((ticks, group)),
            dma((ticks, group)),
            dma((ticks, group)),
            dma((group,)),
            dma((group,)),
        ],
        compiler_params=pltpu.CompilerParams(
            collective_id=0, has_side_effects=True, vmem_limit_bytes=63 * 1024 * 1024
        ),
    )(
        block_in[0],
        fresh_patches,
        jnp.transpose(w_qkv[0], (1, 0, 2)),
        mod_shift,
        mod_scale,
        gate,
        q_gain,
        k_gain,
        image_cache[0],
        text_cache[0],
        patch_order,
        text_length,
    )
    return out[None], cache[None]


def solution(mesh):
    in_specs = (
        P("section", "uly", None),
        P(None, "uly", None),
        P("section", None, None, "uly"),
        P("section", None),
        P("section", None),
        P("section", None),
        P("section", None),
        P("section", None),
        P("section", None, None, "uly"),
        P("section", None, None, "uly"),
        P(),
        P(),
    )
    out_specs = (P("section", "uly", None), P("section", None, None, "uly"))
    return jax.shard_map(body, mesh=mesh, in_specs=in_specs, out_specs=out_specs, check_vma=False)
```

```python
import functools
import math

import jax
import jax.numpy as jnp
from jax import lax
from jax.experimental import pallas as pl
from jax.experimental.pallas import tpu as pltpu
from jax.sharding import PartitionSpec as P

MESH = pl.DeviceIdType.MESH
F32 = jnp.float32
BF16 = jnp.bfloat16
EPS = 1e-06
VMEM_LIMIT = 63 * 1024 * 1024


def head_factor(values):
    return lax.rsqrt(jnp.mean(values * values, axis=-1, keepdims=True) + EPS)


def normed(values, gain, head_dim):
    parts = []
    for start in range(0, values.shape[1], head_dim):
        part = values[:, start : start + head_dim]
        parts.append(part * head_factor(part) * gain)
    return jnp.concatenate(parts, axis=1)


def fold(w, shift, scale, plain_sum, shift_sum, local):
    width = w.shape[1]
    block = 256
    first = lax.broadcasted_iota(jnp.int32, (16, block), 0)
    ones = jnp.ones((16, block), BF16)

    def step(i, totals):
        at = pl.ds(pl.multiple_of(i * block, block), block)
        shift_row = shift[:, at]
        high = shift_row.astype(BF16).astype(F32)
        both = jnp.where(first == 0, high, jnp.where(first == 1, shift_row - high, 0.0))
        both = both.astype(BF16)
        factors = []
        for part in range(block // 128):
            row = scale[:, pl.ds(pl.multiple_of(i * block + part * 128, 128), 128)]
            factors.append(jnp.transpose(jnp.broadcast_to(1.0 + row, (128, 128))))
        factor = jnp.concatenate(factors, axis=0)
        new = []
        for j in range(3):
            rows = w[j, at, :]
            folded = jnp.concatenate(
                [
                    (rows[:, c : c + 128].astype(F32) * factor).astype(BF16)
                    for c in range(0, local, 128)
                ],
                axis=1,
            )
            w[j, at, :] = folded
            new.append(totals[2 * j] + jnp.dot(ones, folded, preferred_element_type=F32))
            new.append(totals[2 * j + 1] + jnp.dot(both, rows, preferred_element_type=F32))
        return tuple(new)

    zero = jnp.zeros((16, local), F32)
    totals = lax.fori_loop(0, width // block, step, (zero,) * 6)
    for j in range(3):
        plain_sum[j] = totals[2 * j][:1]
        shift_sum[j] = totals[2 * j + 1][:1] + totals[2 * j + 1][1:2]


def lanes_summed(values):
    return sum(values[:, c : c + 128] for c in range(0, values.shape[1], 128))


def project(stream, order, arrived, w, plain_sum, shift_sum, local, width):
    near = len(order) // 2
    sums = [None] * 3

    def add(chunk, c):
        at = pl.ds(pl.multiple_of(c * local, local), local)
        for j in range(3):
            product = jnp.dot(chunk, w[j, at, :], preferred_element_type=F32)
            sums[j] = product if sums[j] is None else sums[j] + product

    values = []
    for c in order[:near]:
        arrived(c)
        chunk = stream[c]
        add(chunk, c)
        values.append(chunk.astype(F32))
    pivot = jnp.sum(lanes_summed(sum(values)), axis=-1, keepdims=True) / (near * local)
    off = [value - pivot for value in values]
    first = lanes_summed(sum(off))
    second = lanes_summed(sum(o * o for o in off))
    for c in order[near:]:
        arrived(c)
        chunk = stream[c]
        add(chunk, c)
        o = chunk.astype(F32) - pivot
        first = first + lanes_summed(o)
        second = second + lanes_summed(o * o)
    beyond = jnp.sum(first, axis=-1, keepdims=True) / width
    variance = jnp.sum(second, axis=-1, keepdims=True) / width - beyond * beyond
    factor = lax.rsqrt(variance + EPS)
    mean = pivot + beyond
    return [factor * (sums[j] - mean * plain_sum[j]) + shift_sum[j] for j in range(3)]


def attend(queries, q_row, keys_kept, values_kept, keys_met, values_met, valid, hd):
    txt = valid.shape[1]
    results = []
    for start in range(0, queries.shape[1], hd):
        at = slice(start, start + hd)
        query = queries[:, at]
        factor = head_factor(query) * (1.0 / math.sqrt(hd))
        query = (query * q_row).astype(BF16)
        contract = (((1,), (1,)), ((), ()))
        kept = lax.dot_general(query, keys_kept[:, at], contract, preferred_element_type=F32)
        met = lax.dot_general(query, keys_met[:, at], contract, preferred_element_type=F32)
        kept = jnp.exp(kept * factor)
        met = jnp.exp(met * factor)
        kept = jnp.concatenate([kept[:, :txt] * valid, kept[:, txt:]], axis=1)
        total = jnp.sum(lanes_summed(kept) + lanes_summed(met), axis=-1, keepdims=True)
        mixed = jnp.dot(
            kept.astype(BF16), values_kept[:, at], preferred_element_type=F32
        ) + jnp.dot(met.astype(BF16), values_met[:, at], preferred_element_type=F32)
        results.append(mixed / total)
    return jnp.concatenate(results, axis=1)


def relay_kernel(
    dims,
    block_hbm,
    fresh_hbm,
    w_hbm,
    shift_hbm,
    scale_hbm,
    gate_hbm,
    q_gain_hbm,
    k_gain_hbm,
    image_hbm,
    text_hbm,
    order_hbm,
    length_hbm,
    out_hbm,
    new_hbm,
    block,
    fresh,
    w,
    shift,
    scale,
    gate,
    q_gain,
    k_gain,
    image,
    text,
    order,
    length,
    plain_sum,
    shift_sum,
    keys_kept,
    values_kept,
    keys_met,
    values_met,
    new,
    stream,
    sent,
    row_send,
    row_recv,
    last_send,
    last_recv,
    out,
    load_sem,
    store_sem,
    row_send_sem,
    row_recv_sem,
    tick_send_sem,
    tick_recv_sem,
    last_send_sem,
    last_recv_sem,
):
    sections, group, ticks, patches, pr, width, local, hd, txt = dims
    heads = local // hd
    rows_dev = pr // group
    half = width // 2
    section = lax.axis_index("section")
    uly = lax.axis_index("uly")

    other = uly + 1 - 2 * lax.rem(uly, 2)
    across = [lax.rem(other + k, group) for k in (4, 2, 6, 0)]
    beside = [lax.rem(uly + k, group) for k in (4, 2, 6)]
    peers = across + beside
    nearest_first = [uly, *beside[1:], beside[0], across[3], across[1], across[2], across[0]]

    barrier = pltpu.get_barrier_semaphore()
    for p in peers:
        pl.semaphore_signal(barrier, inc=1, device_id=(section, p), device_id_type=MESH)

    @pl.when(section > 0)
    def _():
        for p in [*peers, uly]:
            pl.semaphore_signal(barrier, inc=1, device_id=(section - 1, p), device_id_type=MESH)

    loads = [
        pltpu.make_async_copy(src, dst, load_sem.at[i])
        for i, (src, dst) in enumerate(
            [
                (block_hbm, block),
                (fresh_hbm, fresh),
                (text_hbm, text),
                (k_gain_hbm, k_gain),
                (image_hbm, image),
                (order_hbm, order),
                (length_hbm, length),
                (shift_hbm, shift),
                (scale_hbm, scale),
                (gate_hbm, gate),
                (q_gain_hbm, q_gain),
                (w_hbm, w),
            ]
        )
    ]
    for copy in loads:
        copy.start()

    loads[0].wait()
    loads[1].wait()
    for t in range(ticks):
        own = block[...] if t == 0 else fresh[t - 1]
        own = own.astype(F32)
        own = jnp.concatenate([own[:, :half], own[:, half:]], axis=0).astype(BF16)
        row_send[t] = own
        row_recv[t, uly] = own

    for copy in loads[2:7]:
        copy.wait()
    k_row = k_gain[...]
    keys_kept[pl.ds(0, txt), :] = normed(text[0].astype(F32), k_row, hd).astype(BF16)
    values_kept[pl.ds(0, txt), :] = text[1]
    for j in range(patches):
        patch = order[lax.rem(j - section + sections * patches, patches)]
        met = []
        for i in range(2):
            rows = image[i, pl.ds(0, pr), :]
            for b in range(1, patches):
                rows = jnp.where(patch == b, image[i, pl.ds(b * pr, pr), :], rows)
            met.append(rows)
        keys, values, at = (
            (keys_met, values_met, pl.ds(j * pr, pr))
            if j < ticks
            else (keys_kept, values_kept, pl.ds(txt + (j - ticks) * pr, pr))
        )
        keys[at, :] = normed(met[0].astype(F32), k_row, hd).astype(BF16)
        values[at, :] = met[1]
    valid = (lax.broadcasted_iota(jnp.int32, (1, txt), 1) < length[0]).astype(F32)

    pl.semaphore_wait(barrier, group - 1 + jnp.where(section < sections - 1, group, 0))

    def row_copy(t, i):
        return pltpu.make_async_remote_copy(
            src_ref=row_send.at[t],
            dst_ref=row_recv.at[t, uly],
            send_sem=row_send_sem.at[t, i],
            recv_sem=row_recv_sem.at[t, uly],
            device_id=(section, peers[i]),
            device_id_type=MESH,
        )

    def row_arrival(t, p):
        return pltpu.make_async_remote_copy(
            src_ref=row_send.at[t],
            dst_ref=row_recv.at[t, p],
            send_sem=row_send_sem.at[t, 0],
            recv_sem=row_recv_sem.at[t, p],
            device_id=(section, p),
            device_id_type=MESH,
        )

    for i in range(group - 1):
        row_copy(0, i).start()

    @pl.when(section == 0)
    def _():
        for t in range(1, ticks):
            for i in range(group - 1):
                row_copy(t, i).start()

    for copy in loads[7:]:
        copy.wait()
    q_row = q_gain[...]
    fold(w, shift, scale, plain_sum, shift_sum, local)

    def rows_to_stream(t):
        for p in peers:
            row_arrival(t, p).wait_recv()
        pieces = [row_recv[t, i].astype(F32) for i in range(group)]
        for side in range(2):
            whole = jnp.concatenate(
                [piece[side * rows_dev : (side + 1) * rows_dev] for piece in pieces], axis=0
            ).astype(BF16)
            for c in range(group // 2):
                stream[t, side * (group // 2) + c] = whole[:, c * local : (c + 1) * local]

    def tick_copy(t, i, p):
        return pltpu.make_async_remote_copy(
            src_ref=sent.at[t],
            dst_ref=stream.at[t + 1, uly],
            send_sem=tick_send_sem.at[t, i],
            recv_sem=tick_recv_sem.at[t + 1, uly],
            device_id=(section + 1, p),
            device_id_type=MESH,
        )

    def tick_arrival(t, p):
        return pltpu.make_async_remote_copy(
            src_ref=sent.at[t],
            dst_ref=stream.at[t, p],
            send_sem=tick_send_sem.at[t, 0],
            recv_sem=tick_recv_sem.at[t, p],
            device_id=(section, uly),
            device_id_type=MESH,
        )

    def last_copy(i):
        return pltpu.make_async_remote_copy(
            src_ref=last_send.at[peers[i]],
            dst_ref=last_recv.at[uly],
            send_sem=last_send_sem.at[i],
            recv_sem=last_recv_sem.at[uly],
            device_id=(section, peers[i]),
            device_id_type=MESH,
        )

    def last_arrival(p):
        return pltpu.make_async_remote_copy(
            src_ref=last_send.at[p],
            dst_ref=last_recv.at[p],
            send_sem=last_send_sem.at[0],
            recv_sem=last_recv_sem.at[p],
            device_id=(section, p),
            device_id_type=MESH,
        )

    own_gate = gate[:, pl.ds(pl.multiple_of(uly * local, local), local)]
    for t in range(ticks):

        @pl.when(section == 0)
        def _():
            rows_to_stream(t)

        if t == 0:

            @pl.when(section > 0)
            def _():
                rows_to_stream(t)

        def arrived(c):
            if t > 0:

                @pl.when(section > 0)
                def _():
                    tick_arrival(t, c).wait_recv()

        queries, new_keys, new_values = project(
            stream.at[t], nearest_first, arrived, w, plain_sum, shift_sum, local, width
        )
        new_keys = new_keys.astype(BF16)
        new_values = new_values.astype(BF16)
        at = pl.ds(t * pr, pr)
        keys_met[at, :] = normed(new_keys.astype(F32), k_row, hd).astype(BF16)
        values_met[at, :] = new_values
        new[0, at, :] = new_keys
        new[1, at, :] = new_values
        attended = attend(
            queries, q_row, keys_kept, values_kept, keys_met, values_met, valid, hd
        )
        result = stream[t, uly].astype(F32) + own_gate * attended.astype(BF16).astype(F32)

        if t < ticks - 1:
            sent[t] = result.astype(BF16)

            @pl.when(section < sections - 1)
            def _():
                for i, p in enumerate([*peers, uly]):
                    tick_copy(t, i, p).start()
        else:
            for i in range(group):
                piece = result[i * rows_dev : (i + 1) * rows_dev]
                last_send[i] = jnp.concatenate(
                    [piece[:, c * hd : (c + 1) * hd] for c in range(heads)], axis=0
                ).astype(BF16)
            for i in range(group - 1):
                last_copy(i).start()
            last_recv[uly] = last_send[uly]

    store = pltpu.make_async_copy(new, new_hbm, store_sem.at[0])
    store.start()
    for i in range(group - 1):
        row_copy(0, i).wait_send()

    @pl.when(section == 0)
    def _():
        for t in range(1, ticks):
            for i in range(group - 1):
                row_copy(t, i).wait_send()

    @pl.when(section < sections - 1)
    def _():
        for t in range(ticks - 1):
            for i, p in enumerate([*peers, uly]):
                tick_copy(t, i, p).wait_send()

    for i in range(group - 1):
        last_copy(i).wait_send()
    store.wait()
    for p in peers:
        last_arrival(p).wait_recv()
    for i in range(group):
        piece = last_recv[i].astype(F32)
        for c in range(heads):
            out[:, pl.ds(i * local + c * hd, hd)] = piece[
                c * rows_dev : (c + 1) * rows_dev
            ].astype(BF16)
    store = pltpu.make_async_copy(out, out_hbm, store_sem.at[1])
    store.start()
    store.wait()


def store_kernel(dims, rows_hbm, new_hbm, image_hbm, order_hbm, out_hbm, cache_hbm, order, sems, order_sem):
    sections, _, ticks, patches, pr, *_ = dims
    section = lax.axis_index("section")
    load = pltpu.make_async_copy(order_hbm, order, order_sem)
    load.start()
    rows = pltpu.make_async_copy(rows_hbm, out_hbm, sems.at[2 * patches])
    rows.start()
    load.wait()
    met = [order[lax.rem(j - section + sections * patches, patches)] for j in range(ticks)]
    for b in range(patches):
        at = pl.ds(b * pr, pr)
        tick = jnp.int32(-1)
        for j in range(ticks):
            tick = jnp.where(met[j] == b, j, tick)

        @pl.when(tick >= 0)
        def _():
            start = pl.multiple_of(tick * pr, pr)
            for i in range(2):
                pltpu.make_async_copy(
                    new_hbm.at[i, pl.ds(start, pr), :], cache_hbm.at[i, at, :], sems.at[2 * b + i]
                ).start()

        @pl.when(tick < 0)
        def _():
            for i in range(2):
                pltpu.make_async_copy(
                    image_hbm.at[i, at, :], cache_hbm.at[i, at, :], sems.at[2 * b + i]
                ).start()

    rows.wait()
    for b in range(patches):
        at = pl.ds(b * pr, pr)
        for i in range(2):
            pltpu.make_async_copy(
                image_hbm.at[i, at, :], cache_hbm.at[i, at, :], sems.at[2 * b + i]
            ).wait()


def body(
    block_in,
    fresh_patches,
    w_qkv,
    mod_shift,
    mod_scale,
    gate,
    q_gain,
    k_gain,
    image_cache,
    text_cache,
    patch_order,
    text_length,
):
    sections, group = lax.axis_size("section"), lax.axis_size("uly")
    rows_dev, width = block_in.shape[1:]
    local = w_qkv.shape[3]
    hd = q_gain.shape[1]
    patches = patch_order.shape[0]
    ticks = fresh_patches.shape[0] + 1
    pr = rows_dev * group
    txt = text_cache.shape[2]
    img = patches * pr
    heads = local // hd
    kept = txt + (patches - ticks) * pr
    dims = (sections, group, ticks, patches, pr, width, local, hd, txt)
    hbm = pl.BlockSpec(memory_space=pl.ANY)
    dma = pltpu.SemaphoreType.DMA
    vmem = pltpu.VMEM
    rows, new = pl.pallas_call(
        functools.partial(relay_kernel, dims),
        out_shape=(
            jax.ShapeDtypeStruct((rows_dev, width), BF16),
            jax.ShapeDtypeStruct((2, ticks * pr, local), BF16),
        ),
        in_specs=[hbm] * 12,
        out_specs=(hbm, hbm),
        scratch_shapes=[
            vmem((rows_dev, width), BF16),
            vmem((ticks - 1, rows_dev, width), BF16),
            vmem((3, width, local), BF16),
            vmem((1, width), F32),
            vmem((1, width), F32),
            vmem((1, width), F32),
            vmem((1, hd), F32),
            vmem((1, hd), F32),
            vmem((2, img, local), BF16),
            vmem((2, txt, local), BF16),
            pltpu.SMEM((patches,), jnp.int32),
            pltpu.SMEM((1,), jnp.int32),
            vmem((3, 1, local), F32),
            vmem((3, 1, local), F32),
            vmem((kept, local), BF16),
            vmem((kept, local), BF16),
            vmem((ticks * pr, local), BF16),
            vmem((ticks * pr, local), BF16),
            vmem((2, ticks * pr, local), BF16),
            vmem((ticks, group, pr, local), BF16),
            vmem((ticks, pr, local), BF16),
            vmem((ticks, 2 * rows_dev, width // 2), BF16),
            vmem((ticks, group, 2 * rows_dev, width // 2), BF16),
            vmem((group, heads * rows_dev, hd), BF16),
            vmem((group, heads * rows_dev, hd), BF16),
            vmem((rows_dev, width), BF16),
            dma((12,)),
            dma((2,)),
            dma((ticks, group)),
            dma((ticks, group)),
            dma((ticks, group)),
            dma((ticks, group)),
            dma((group,)),
            dma((group,)),
        ],
        compiler_params=pltpu.CompilerParams(
            collective_id=0, has_side_effects=True, vmem_limit_bytes=VMEM_LIMIT
        ),
        name="relay",
    )(
        block_in[0],
        fresh_patches,
        jnp.transpose(w_qkv[0], (1, 0, 2)),
        mod_shift,
        mod_scale,
        gate,
        q_gain,
        k_gain,
        image_cache[0],
        text_cache[0],
        patch_order,
        text_length,
    )
    out, cache = pl.pallas_call(
        functools.partial(store_kernel, dims),
        out_shape=(
            jax.ShapeDtypeStruct((rows_dev, width), BF16),
            jax.ShapeDtypeStruct((2, img, local), BF16),
        ),
        in_specs=[hbm] * 4,
        out_specs=(hbm, hbm),
        scratch_shapes=[
            pltpu.SMEM((patches,), jnp.int32),
            dma((2 * patches + 1,)),
            dma,
        ],
        compiler_params=pltpu.CompilerParams(vmem_limit_bytes=VMEM_LIMIT),
        name="outputs",
    )(rows, new, image_cache[0], patch_order)
    return out[None], cache[None]


def solution(mesh):
    in_specs = (
        P("section", "uly", None),
        P(None, "uly", None),
        P("section", None, None, "uly"),
        P("section", None),
        P("section", None),
        P("section", None),
        P("section", None),
        P("section", None),
        P("section", None, None, "uly"),
        P("section", None, None, "uly"),
        P(),
        P(),
    )
    out_specs = (P("section", "uly", None), P("section", None, None, "uly"))
    return jax.shard_map(body, mesh=mesh, in_specs=in_specs, out_specs=out_specs, check_vma=False)
```

```python
import functools
import math

import jax
import jax.numpy as jnp
from jax import lax
from jax.experimental import pallas as pl
from jax.experimental.pallas import tpu as pltpu
from jax.sharding import PartitionSpec as P

MESH = pl.DeviceIdType.MESH
F32 = jnp.float32
BF16 = jnp.bfloat16
EPS = 1e-06
VMEM_LIMIT = 63 * 1024 * 1024


def head_factor(values):
    return lax.rsqrt(jnp.mean(values * values, axis=-1, keepdims=True) + EPS)


def normed(values, gain, head_dim):
    parts = []
    for start in range(0, values.shape[1], head_dim):
        part = values[:, start : start + head_dim]
        parts.append(part * head_factor(part) * gain)
    return jnp.concatenate(parts, axis=1)


def fold(w, shift, scale, plain_sum, shift_sum, local):
    width = w.shape[1]
    block = 256
    first = lax.broadcasted_iota(jnp.int32, (16, block), 0)
    ones = jnp.ones((16, block), BF16)

    def step(i, totals):
        at = pl.ds(pl.multiple_of(i * block, block), block)
        shift_row = shift[:, at]
        high = shift_row.astype(BF16).astype(F32)
        both = jnp.where(first == 0, high, jnp.where(first == 1, shift_row - high, 0.0))
        both = both.astype(BF16)
        factors = []
        for part in range(block // 128):
            row = scale[:, pl.ds(pl.multiple_of(i * block + part * 128, 128), 128)]
            factors.append(jnp.transpose(jnp.broadcast_to(1.0 + row, (128, 128))))
        factor = jnp.concatenate(factors, axis=0)
        new = []
        for j in range(3):
            rows = w[j, at, :]
            folded = jnp.concatenate(
                [
                    (rows[:, c : c + 128].astype(F32) * factor).astype(BF16)
                    for c in range(0, local, 128)
                ],
                axis=1,
            )
            w[j, at, :] = folded
            new.append(totals[2 * j] + jnp.dot(ones, folded, preferred_element_type=F32))
            new.append(totals[2 * j + 1] + jnp.dot(both, rows, preferred_element_type=F32))
        return tuple(new)

    zero = jnp.zeros((16, local), F32)
    totals = lax.fori_loop(0, width // block, step, (zero,) * 6)
    for j in range(3):
        plain_sum[j] = totals[2 * j][:1]
        shift_sum[j] = totals[2 * j + 1][:1] + totals[2 * j + 1][1:2]


def lanes_summed(values):
    return sum(values[:, c : c + 128] for c in range(0, values.shape[1], 128))


def project(stream, order, arrived, w, plain_sum, shift_sum, local, width):
    near = len(order) // 2
    sums = [None] * 3

    def add(chunk, c):
        at = pl.ds(pl.multiple_of(c * local, local), local)
        for j in range(3):
            product = jnp.dot(chunk, w[j, at, :], preferred_element_type=F32)
            sums[j] = product if sums[j] is None else sums[j] + product

    values = []
    for c in order[:near]:
        arrived(c)
        chunk = stream[c]
        add(chunk, c)
        values.append(chunk.astype(F32))
    pivot = jnp.sum(lanes_summed(sum(values)), axis=-1, keepdims=True) / (near * local)
    off = [value - pivot for value in values]
    first = lanes_summed(sum(off))
    second = lanes_summed(sum(o * o for o in off))
    for c in order[near:]:
        arrived(c)
        chunk = stream[c]
        add(chunk, c)
        o = chunk.astype(F32) - pivot
        first = first + lanes_summed(o)
        second = second + lanes_summed(o * o)
    beyond = jnp.sum(first, axis=-1, keepdims=True) / width
    variance = jnp.sum(second, axis=-1, keepdims=True) / width - beyond * beyond
    factor = lax.rsqrt(variance + EPS)
    mean = pivot + beyond
    return [factor * (sums[j] - mean * plain_sum[j]) + shift_sum[j] for j in range(3)]


def attend(queries, q_row, keys_kept, values_kept, keys_met, values_met, valid, hd):
    rows, txt = queries.shape[0], valid.shape[1]
    heads = queries.shape[1] // hd
    stacked, factors = [], []
    for h in range(heads):
        query = queries[:, h * hd : (h + 1) * hd]
        factors.append(head_factor(query) * (1.0 / math.sqrt(hd)))
        parts = [jnp.zeros((rows, hd), BF16)] * heads
        parts[h] = (query * q_row).astype(BF16)
        stacked.append(jnp.concatenate(parts, axis=1))
    stacked = jnp.concatenate(stacked, axis=0)
    factor = jnp.concatenate(factors, axis=0)
    contract = (((1,), (1,)), ((), ()))
    kept = lax.dot_general(stacked, keys_kept[...], contract, preferred_element_type=F32)
    met = lax.dot_general(stacked, keys_met[...], contract, preferred_element_type=F32)
    kept = jnp.exp(kept * factor)
    met = jnp.exp(met * factor)
    kept = jnp.concatenate([kept[:, :txt] * valid, kept[:, txt:]], axis=1)
    total = jnp.sum(lanes_summed(kept) + lanes_summed(met), axis=-1, keepdims=True)
    mixed = jnp.dot(
        kept.astype(BF16), values_kept[...], preferred_element_type=F32
    ) + jnp.dot(met.astype(BF16), values_met[...], preferred_element_type=F32)
    mixed = mixed / total
    return jnp.concatenate(
        [mixed[h * rows : (h + 1) * rows, h * hd : (h + 1) * hd] for h in range(heads)], axis=1
    )


def relay_kernel(
    dims,
    block_hbm,
    fresh_hbm,
    w_hbm,
    shift_hbm,
    scale_hbm,
    gate_hbm,
    q_gain_hbm,
    k_gain_hbm,
    image_hbm,
    text_hbm,
    order_hbm,
    length_hbm,
    out_hbm,
    new_hbm,
    block,
    fresh,
    w,
    shift,
    scale,
    gate,
    q_gain,
    k_gain,
    image,
    text,
    order,
    length,
    plain_sum,
    shift_sum,
    keys_kept,
    values_kept,
    keys_met,
    values_met,
    new,
    stream,
    sent,
    row_send,
    row_recv,
    last_send,
    last_recv,
    out,
    load_sem,
    store_sem,
    row_send_sem,
    row_recv_sem,
    tick_send_sem,
    tick_recv_sem,
    last_send_sem,
    last_recv_sem,
):
    sections, group, ticks, patches, pr, width, local, hd, txt = dims
    heads = local // hd
    rows_dev = pr // group
    half = width // 2
    section = lax.axis_index("section")
    uly = lax.axis_index("uly")

    other = uly + 1 - 2 * lax.rem(uly, 2)
    across = [lax.rem(other + k, group) for k in (4, 2, 6, 0)]
    beside = [lax.rem(uly + k, group) for k in (4, 2, 6)]
    peers = across + beside
    nearest_first = [uly, *beside[1:], beside[0], across[3], across[1], across[2], across[0]]

    barrier = pltpu.get_barrier_semaphore()
    for p in peers:
        pl.semaphore_signal(barrier, inc=1, device_id=(section, p), device_id_type=MESH)

    @pl.when(section > 0)
    def _():
        for p in [*peers, uly]:
            pl.semaphore_signal(barrier, inc=1, device_id=(section - 1, p), device_id_type=MESH)

    loads = [
        pltpu.make_async_copy(src, dst, load_sem.at[i])
        for i, (src, dst) in enumerate(
            [
                (block_hbm, block),
                (fresh_hbm, fresh),
                (text_hbm, text),
                (k_gain_hbm, k_gain),
                (image_hbm, image),
                (order_hbm, order),
                (length_hbm, length),
                (shift_hbm, shift),
                (scale_hbm, scale),
                (gate_hbm, gate),
                (q_gain_hbm, q_gain),
                (w_hbm, w),
            ]
        )
    ]
    for copy in loads:
        copy.start()

    loads[0].wait()
    loads[1].wait()
    for t in range(ticks):
        own = block[...] if t == 0 else fresh[t - 1]
        own = own.astype(F32)
        own = jnp.concatenate([own[:, :half], own[:, half:]], axis=0).astype(BF16)
        row_send[t] = own
        row_recv[t, uly] = own

    for copy in loads[2:7]:
        copy.wait()
    k_row = k_gain[...]
    keys_kept[pl.ds(0, txt), :] = normed(text[0].astype(F32), k_row, hd).astype(BF16)
    values_kept[pl.ds(0, txt), :] = text[1]
    for j in range(patches):
        patch = order[lax.rem(j - section + sections * patches, patches)]
        met = []
        for i in range(2):
            rows = image[i, pl.ds(0, pr), :]
            for b in range(1, patches):
                rows = jnp.where(patch == b, image[i, pl.ds(b * pr, pr), :], rows)
            met.append(rows)
        keys, values, at = (
            (keys_met, values_met, pl.ds(j * pr, pr))
            if j < ticks
            else (keys_kept, values_kept, pl.ds(txt + (j - ticks) * pr, pr))
        )
        keys[at, :] = normed(met[0].astype(F32), k_row, hd).astype(BF16)
        values[at, :] = met[1]
    valid = (lax.broadcasted_iota(jnp.int32, (1, txt), 1) < length[0]).astype(F32)

    pl.semaphore_wait(barrier, group - 1 + jnp.where(section < sections - 1, group, 0))

    def row_copy(t, i):
        return pltpu.make_async_remote_copy(
            src_ref=row_send.at[t],
            dst_ref=row_recv.at[t, uly],
            send_sem=row_send_sem.at[t, i],
            recv_sem=row_recv_sem.at[t, uly],
            device_id=(section, peers[i]),
            device_id_type=MESH,
        )

    def row_arrival(t, p):
        return pltpu.make_async_remote_copy(
            src_ref=row_send.at[t],
            dst_ref=row_recv.at[t, p],
            send_sem=row_send_sem.at[t, 0],
            recv_sem=row_recv_sem.at[t, p],
            device_id=(section, p),
            device_id_type=MESH,
        )

    for i in range(group - 1):
        row_copy(0, i).start()

    @pl.when(section == 0)
    def _():
        for t in range(1, ticks):
            for i in range(group - 1):
                row_copy(t, i).start()

    for copy in loads[7:]:
        copy.wait()
    q_row = q_gain[...]
    fold(w, shift, scale, plain_sum, shift_sum, local)

    def rows_to_stream(t):
        for p in peers:
            row_arrival(t, p).wait_recv()
        pieces = [row_recv[t, i].astype(F32) for i in range(group)]
        for side in range(2):
            whole = jnp.concatenate(
                [piece[side * rows_dev : (side + 1) * rows_dev] for piece in pieces], axis=0
            ).astype(BF16)
            for c in range(group // 2):
                stream[t, side * (group // 2) + c] = whole[:, c * local : (c + 1) * local]

    def tick_copy(t, i, p):
        return pltpu.make_async_remote_copy(
            src_ref=sent.at[t],
            dst_ref=stream.at[t + 1, uly],
            send_sem=tick_send_sem.at[t, i],
            recv_sem=tick_recv_sem.at[t + 1, uly],
            device_id=(section + 1, p),
            device_id_type=MESH,
        )

    def tick_arrival(t, p):
        return pltpu.make_async_remote_copy(
            src_ref=sent.at[t],
            dst_ref=stream.at[t, p],
            send_sem=tick_send_sem.at[t, 0],
            recv_sem=tick_recv_sem.at[t, p],
            device_id=(section, uly),
            device_id_type=MESH,
        )

    def last_copy(i):
        return pltpu.make_async_remote_copy(
            src_ref=last_send.at[peers[i]],
            dst_ref=last_recv.at[uly],
            send_sem=last_send_sem.at[i],
            recv_sem=last_recv_sem.at[uly],
            device_id=(section, peers[i]),
            device_id_type=MESH,
        )

    def last_arrival(p):
        return pltpu.make_async_remote_copy(
            src_ref=last_send.at[p],
            dst_ref=last_recv.at[p],
            send_sem=last_send_sem.at[0],
            recv_sem=last_recv_sem.at[p],
            device_id=(section, p),
            device_id_type=MESH,
        )

    own_gate = gate[:, pl.ds(pl.multiple_of(uly * local, local), local)]
    for t in range(ticks):

        @pl.when(section == 0)
        def _():
            rows_to_stream(t)

        if t == 0:

            @pl.when(section > 0)
            def _():
                rows_to_stream(t)

        def arrived(c):
            if t > 0:

                @pl.when(section > 0)
                def _():
                    tick_arrival(t, c).wait_recv()

        queries, new_keys, new_values = project(
            stream.at[t], nearest_first, arrived, w, plain_sum, shift_sum, local, width
        )
        new_keys = new_keys.astype(BF16)
        new_values = new_values.astype(BF16)
        at = pl.ds(t * pr, pr)
        keys_met[at, :] = normed(new_keys.astype(F32), k_row, hd).astype(BF16)
        values_met[at, :] = new_values
        new[0, at, :] = new_keys
        new[1, at, :] = new_values
        attended = attend(
            queries, q_row, keys_kept, values_kept, keys_met, values_met, valid, hd
        )
        result = stream[t, uly].astype(F32) + own_gate * attended.astype(BF16).astype(F32)

        if t < ticks - 1:
            sent[t] = result.astype(BF16)

            @pl.when(section < sections - 1)
            def _():
                for i, p in enumerate([*peers, uly]):
                    tick_copy(t, i, p).start()
        else:
            for i in range(group):
                piece = result[i * rows_dev : (i + 1) * rows_dev]
                last_send[i] = jnp.concatenate(
                    [piece[:, c * hd : (c + 1) * hd] for c in range(heads)], axis=0
                ).astype(BF16)
            for i in range(group - 1):
                last_copy(i).start()
            last_recv[uly] = last_send[uly]

    store = pltpu.make_async_copy(new, new_hbm, store_sem.at[0])
    store.start()
    for i in range(group - 1):
        row_copy(0, i).wait_send()

    @pl.when(section == 0)
    def _():
        for t in range(1, ticks):
            for i in range(group - 1):
                row_copy(t, i).wait_send()

    @pl.when(section < sections - 1)
    def _():
        for t in range(ticks - 1):
            for i, p in enumerate([*peers, uly]):
                tick_copy(t, i, p).wait_send()

    for i in range(group - 1):
        last_copy(i).wait_send()
    store.wait()
    for p in peers:
        last_arrival(p).wait_recv()
    for i in range(group):
        piece = last_recv[i].astype(F32)
        for c in range(heads):
            out[:, pl.ds(i * local + c * hd, hd)] = piece[
                c * rows_dev : (c + 1) * rows_dev
            ].astype(BF16)
    store = pltpu.make_async_copy(out, out_hbm, store_sem.at[1])
    store.start()
    store.wait()


def store_kernel(
    dims, rows_hbm, new_hbm, image_hbm, order_hbm, out_hbm, cache_hbm, rows, new, cache, order, load_sem, store_sem
):
    sections, _, ticks, patches, pr, *_ = dims
    section = lax.axis_index("section")
    loads = [
        pltpu.make_async_copy(src, dst, load_sem.at[i])
        for i, (src, dst) in enumerate(
            [
                (order_hbm, order),
                (image_hbm.at[0], cache.at[0]),
                (image_hbm.at[1], cache.at[1]),
                (new_hbm, new),
                (rows_hbm, rows),
            ]
        )
    ]
    for copy in loads:
        copy.start()
    stores = [
        pltpu.make_async_copy(src, dst, store_sem.at[i])
        for i, (src, dst) in enumerate(
            [
                (cache.at[0], cache_hbm.at[0]),
                (cache.at[1], cache_hbm.at[1]),
                (rows, out_hbm),
            ]
        )
    ]
    loads[4].wait()
    stores[2].start()
    loads[0].wait()
    met = [order[lax.rem(j - section + sections * patches, patches)] for j in range(ticks)]
    loads[3].wait()
    for i in range(2):
        loads[1 + i].wait()
        for j in range(ticks):
            at = pl.ds(pl.multiple_of(met[j] * pr, pr), pr)
            cache[i, at, :] = new[i, pl.ds(j * pr, pr), :]
        stores[i].start()
    for copy in stores:
        copy.wait()


def body(
    block_in,
    fresh_patches,
    w_qkv,
    mod_shift,
    mod_scale,
    gate,
    q_gain,
    k_gain,
    image_cache,
    text_cache,
    patch_order,
    text_length,
):
    sections, group = lax.axis_size("section"), lax.axis_size("uly")
    rows_dev, width = block_in.shape[1:]
    local = w_qkv.shape[3]
    hd = q_gain.shape[1]
    patches = patch_order.shape[0]
    ticks = fresh_patches.shape[0] + 1
    pr = rows_dev * group
    txt = text_cache.shape[2]
    img = patches * pr
    heads = local // hd
    kept = txt + (patches - ticks) * pr
    dims = (sections, group, ticks, patches, pr, width, local, hd, txt)
    hbm = pl.BlockSpec(memory_space=pl.ANY)
    dma = pltpu.SemaphoreType.DMA
    vmem = pltpu.VMEM
    rows, new = pl.pallas_call(
        functools.partial(relay_kernel, dims),
        out_shape=(
            jax.ShapeDtypeStruct((rows_dev, width), BF16),
            jax.ShapeDtypeStruct((2, ticks * pr, local), BF16),
        ),
        in_specs=[hbm] * 12,
        out_specs=(hbm, hbm),
        scratch_shapes=[
            vmem((rows_dev, width), BF16),
            vmem((ticks - 1, rows_dev, width), BF16),
            vmem((3, width, local), BF16),
            vmem((1, width), F32),
            vmem((1, width), F32),
            vmem((1, width), F32),
            vmem((1, hd), F32),
            vmem((1, hd), F32),
            vmem((2, img, local), BF16),
            vmem((2, txt, local), BF16),
            pltpu.SMEM((patches,), jnp.int32),
            pltpu.SMEM((1,), jnp.int32),
            vmem((3, 1, local), F32),
            vmem((3, 1, local), F32),
            vmem((kept, local), BF16),
            vmem((kept, local), BF16),
            vmem((ticks * pr, local), BF16),
            vmem((ticks * pr, local), BF16),
            vmem((2, ticks * pr, local), BF16),
            vmem((ticks, group, pr, local), BF16),
            vmem((ticks, pr, local), BF16),
            vmem((ticks, 2 * rows_dev, width // 2), BF16),
            vmem((ticks, group, 2 * rows_dev, width // 2), BF16),
            vmem((group, heads * rows_dev, hd), BF16),
            vmem((group, heads * rows_dev, hd), BF16),
            vmem((rows_dev, width), BF16),
            dma((12,)),
            dma((2,)),
            dma((ticks, group)),
            dma((ticks, group)),
            dma((ticks, group)),
            dma((ticks, group)),
            dma((group,)),
            dma((group,)),
        ],
        compiler_params=pltpu.CompilerParams(
            collective_id=0, has_side_effects=True, vmem_limit_bytes=VMEM_LIMIT
        ),
        name="relay",
    )(
        block_in[0],
        fresh_patches,
        jnp.transpose(w_qkv[0], (1, 0, 2)),
        mod_shift,
        mod_scale,
        gate,
        q_gain,
        k_gain,
        image_cache[0],
        text_cache[0],
        patch_order,
        text_length,
    )
    out, cache = pl.pallas_call(
        functools.partial(store_kernel, dims),
        out_shape=(
            jax.ShapeDtypeStruct((rows_dev, width), BF16),
            jax.ShapeDtypeStruct((2, img, local), BF16),
        ),
        in_specs=[hbm] * 4,
        out_specs=(hbm, hbm),
        scratch_shapes=[
            vmem((rows_dev, width), BF16),
            vmem((2, ticks * pr, local), BF16),
            vmem((2, img, local), BF16),
            pltpu.SMEM((patches,), jnp.int32),
            dma((5,)),
            dma((3,)),
        ],
        compiler_params=pltpu.CompilerParams(vmem_limit_bytes=VMEM_LIMIT),
        name="outputs",
    )(rows, new, image_cache[0], patch_order)
    return out[None], cache[None]


def solution(mesh):
    in_specs = (
        P("section", "uly", None),
        P(None, "uly", None),
        P("section", None, None, "uly"),
        P("section", None),
        P("section", None),
        P("section", None),
        P("section", None),
        P("section", None),
        P("section", None, None, "uly"),
        P("section", None, None, "uly"),
        P(),
        P(),
    )
    out_specs = (P("section", "uly", None), P("section", None, None, "uly"))
    return jax.shard_map(body, mesh=mesh, in_specs=in_specs, out_specs=out_specs, check_vma=False)
```

```python
import functools
import math

import jax
import jax.numpy as jnp
from jax import lax
from jax.experimental import pallas as pl
from jax.experimental.pallas import tpu as pltpu
from jax.sharding import PartitionSpec as P

MESH = pl.DeviceIdType.MESH
F32 = jnp.float32
BF16 = jnp.bfloat16
EPS = 1e-06
VMEM_LIMIT = 48 * 1024 * 1024


def head_factor(values):
    return lax.rsqrt(jnp.mean(values * values, axis=-1, keepdims=True) + EPS)


def normed(values, gain, head_dim):
    parts = []
    for start in range(0, values.shape[1], head_dim):
        part = values[:, start : start + head_dim]
        parts.append(part * head_factor(part) * gain)
    return jnp.concatenate(parts, axis=1)


def fold(w, shift, scale, plain_sum, shift_sum, local):
    width = w.shape[1]
    block = 256
    first = lax.broadcasted_iota(jnp.int32, (16, block), 0)
    ones = jnp.ones((16, block), BF16)

    def step(i, totals):
        at = pl.ds(pl.multiple_of(i * block, block), block)
        shift_row = shift[:, at]
        high = shift_row.astype(BF16).astype(F32)
        both = jnp.where(first == 0, high, jnp.where(first == 1, shift_row - high, 0.0))
        both = both.astype(BF16)
        factors = []
        for part in range(block // 128):
            row = scale[:, pl.ds(pl.multiple_of(i * block + part * 128, 128), 128)]
            factors.append(jnp.transpose(jnp.broadcast_to(1.0 + row, (128, 128))))
        factor = jnp.concatenate(factors, axis=0)
        new = []
        for j in range(3):
            rows = w[j, at, :]
            folded = jnp.concatenate(
                [
                    (rows[:, c : c + 128].astype(F32) * factor).astype(BF16)
                    for c in range(0, local, 128)
                ],
                axis=1,
            )
            w[j, at, :] = folded
            new.append(totals[2 * j] + jnp.dot(ones, folded, preferred_element_type=F32))
            new.append(totals[2 * j + 1] + jnp.dot(both, rows, preferred_element_type=F32))
        return tuple(new)

    zero = jnp.zeros((16, local), F32)
    totals = lax.fori_loop(0, width // block, step, (zero,) * 6)
    for j in range(3):
        plain_sum[j] = totals[2 * j][:1]
        shift_sum[j] = totals[2 * j + 1][:1] + totals[2 * j + 1][1:2]


def lanes_summed(values):
    return sum(values[:, c : c + 128] for c in range(0, values.shape[1], 128))


def project(stream, order, arrived, w, plain_sum, shift_sum, local, width):
    near = len(order) // 2
    sums = [None] * 3

    def add(chunk, c):
        at = pl.ds(pl.multiple_of(c * local, local), local)
        for j in range(3):
            product = jnp.dot(chunk, w[j, at, :], preferred_element_type=F32)
            sums[j] = product if sums[j] is None else sums[j] + product

    values = []
    for c in order[:near]:
        arrived(c)
        chunk = stream[c]
        add(chunk, c)
        values.append(chunk.astype(F32))
    pivot = jnp.sum(lanes_summed(sum(values)), axis=-1, keepdims=True) / (near * local)
    off = [value - pivot for value in values]
    first = lanes_summed(sum(off))
    second = lanes_summed(sum(o * o for o in off))
    for c in order[near:]:
        arrived(c)
        chunk = stream[c]
        add(chunk, c)
        o = chunk.astype(F32) - pivot
        first = first + lanes_summed(o)
        second = second + lanes_summed(o * o)
    beyond = jnp.sum(first, axis=-1, keepdims=True) / width
    variance = jnp.sum(second, axis=-1, keepdims=True) / width - beyond * beyond
    factor = lax.rsqrt(variance + EPS)
    mean = pivot + beyond
    return [factor * (sums[j] - mean * plain_sum[j]) + shift_sum[j] for j in range(3)]


def attend(queries, q_row, keys_kept, values_kept, keys_met, values_met, valid, hd):
    rows, txt = queries.shape[0], valid.shape[1]
    heads = queries.shape[1] // hd
    stacked, factors = [], []
    for h in range(heads):
        query = queries[:, h * hd : (h + 1) * hd]
        factors.append(head_factor(query) * (1.0 / math.sqrt(hd)))
        parts = [jnp.zeros((rows, hd), BF16)] * heads
        parts[h] = (query * q_row).astype(BF16)
        stacked.append(jnp.concatenate(parts, axis=1))
    stacked = jnp.concatenate(stacked, axis=0)
    factor = jnp.concatenate(factors, axis=0)
    contract = (((1,), (1,)), ((), ()))
    kept = lax.dot_general(stacked, keys_kept[...], contract, preferred_element_type=F32)
    met = lax.dot_general(stacked, keys_met[...], contract, preferred_element_type=F32)
    kept = jnp.exp(kept * factor)
    met = jnp.exp(met * factor)
    kept = jnp.concatenate([kept[:, :txt] * valid, kept[:, txt:]], axis=1)
    total = jnp.sum(lanes_summed(kept) + lanes_summed(met), axis=-1, keepdims=True)
    mixed = jnp.dot(
        kept.astype(BF16), values_kept[...], preferred_element_type=F32
    ) + jnp.dot(met.astype(BF16), values_met[...], preferred_element_type=F32)
    mixed = mixed / total
    return jnp.concatenate(
        [mixed[h * rows : (h + 1) * rows, h * hd : (h + 1) * hd] for h in range(heads)], axis=1
    )


def relay_kernel(
    dims,
    block_hbm,
    fresh_hbm,
    w_hbm,
    shift_hbm,
    scale_hbm,
    gate_hbm,
    q_gain_hbm,
    k_gain_hbm,
    image_hbm,
    text_hbm,
    order_hbm,
    length_hbm,
    out,
    cache_out,
    block,
    fresh,
    w,
    shift,
    scale,
    gate,
    q_gain,
    k_gain,
    image,
    text,
    order,
    length,
    plain_sum,
    shift_sum,
    keys_kept,
    values_kept,
    keys_met,
    values_met,
    new,
    stream,
    sent,
    row_send,
    row_recv,
    last_send,
    last_recv,
    load_sem,
    row_send_sem,
    row_recv_sem,
    tick_send_sem,
    tick_recv_sem,
    last_send_sem,
    last_recv_sem,
):
    sections, group, ticks, patches, pr, width, local, hd, txt = dims
    heads = local // hd
    rows_dev = pr // group
    half = width // 2
    section = lax.axis_index("section")
    uly = lax.axis_index("uly")

    other = uly + 1 - 2 * lax.rem(uly, 2)
    across = [lax.rem(other + k, group) for k in (4, 2, 6, 0)]
    beside = [lax.rem(uly + k, group) for k in (4, 2, 6)]
    peers = [across[0], beside[0], across[1], beside[1], across[2], beside[2], across[3]]
    nearest_first = [uly, *beside[1:], beside[0], across[3], across[1], across[2], across[0]]

    barrier = pltpu.get_barrier_semaphore()
    for p in peers:
        pl.semaphore_signal(barrier, inc=1, device_id=(section, p), device_id_type=MESH)

    @pl.when(section > 0)
    def _():
        for p in [*peers, uly]:
            pl.semaphore_signal(barrier, inc=1, device_id=(section - 1, p), device_id_type=MESH)

    loads = [
        pltpu.make_async_copy(src, dst, load_sem.at[i])
        for i, (src, dst) in enumerate(
            [
                (block_hbm, block),
                (fresh_hbm, fresh),
                (text_hbm, text),
                (k_gain_hbm, k_gain),
                (image_hbm, image),
                (order_hbm, order),
                (length_hbm, length),
                (shift_hbm, shift),
                (scale_hbm, scale),
                (gate_hbm, gate),
                (q_gain_hbm, q_gain),
                (w_hbm, w),
            ]
        )
    ]
    for copy in loads:
        copy.start()

    loads[0].wait()
    loads[1].wait()
    for t in range(ticks):
        own = block[...] if t == 0 else fresh[t - 1]
        own = own.astype(F32)
        own = jnp.concatenate([own[:, :half], own[:, half:]], axis=0).astype(BF16)
        row_send[t] = own
        row_recv[t, uly] = own

    def patch_at(slot):
        return order[lax.rem(slot - section + sections * patches, patches)]

    for copy in loads[2:7]:
        copy.wait()
    k_row = k_gain[...]
    keys_kept[pl.ds(0, txt), :] = normed(text[0].astype(F32), k_row, hd).astype(BF16)
    values_kept[pl.ds(0, txt), :] = text[1]
    for j in range(patches):
        patch = patch_at(j)
        met = []
        for i in range(2):
            rows = image[i, pl.ds(0, pr), :]
            for b in range(1, patches):
                rows = jnp.where(patch == b, image[i, pl.ds(b * pr, pr), :], rows)
            met.append(rows)
        keys, values, at = (
            (keys_met, values_met, pl.ds(j * pr, pr))
            if j < ticks
            else (keys_kept, values_kept, pl.ds(txt + (j - ticks) * pr, pr))
        )
        keys[at, :] = normed(met[0].astype(F32), k_row, hd).astype(BF16)
        values[at, :] = met[1]
    valid = (lax.broadcasted_iota(jnp.int32, (1, txt), 1) < length[0]).astype(F32)

    pl.semaphore_wait(barrier, group - 1 + jnp.where(section < sections - 1, group, 0))

    def row_copy(t, i):
        return pltpu.make_async_remote_copy(
            src_ref=row_send.at[t],
            dst_ref=row_recv.at[t, uly],
            send_sem=row_send_sem.at[t, i],
            recv_sem=row_recv_sem.at[t, uly],
            device_id=(section, peers[i]),
            device_id_type=MESH,
        )

    def row_arrival(t, p):
        return pltpu.make_async_remote_copy(
            src_ref=row_send.at[t],
            dst_ref=row_recv.at[t, p],
            send_sem=row_send_sem.at[t, 0],
            recv_sem=row_recv_sem.at[t, p],
            device_id=(section, p),
            device_id_type=MESH,
        )

    for copy in loads[7:]:
        copy.wait()
    q_row = q_gain[...]
    even = lax.rem(section, 2) == 0

    @pl.when(even)
    def _():
        fold(w, shift, scale, plain_sum, shift_sum, local)

    for i in range(group - 1):
        row_copy(0, i).start()

    @pl.when(section == 0)
    def _():
        for t in range(1, ticks):
            for i in range(group - 1):
                row_copy(t, i).start()

    @pl.when(jnp.logical_not(even))
    def _():
        fold(w, shift, scale, plain_sum, shift_sum, local)

    def rows_to_stream(t):
        for p in peers:
            row_arrival(t, p).wait_recv()
        pieces = [row_recv[t, i].astype(F32) for i in range(group)]
        for side in range(2):
            whole = jnp.concatenate(
                [piece[side * rows_dev : (side + 1) * rows_dev] for piece in pieces], axis=0
            ).astype(BF16)
            for c in range(group // 2):
                stream[t, side * (group // 2) + c] = whole[:, c * local : (c + 1) * local]

    def tick_copy(t, i, p):
        return pltpu.make_async_remote_copy(
            src_ref=sent.at[t],
            dst_ref=stream.at[t + 1, uly],
            send_sem=tick_send_sem.at[t, i],
            recv_sem=tick_recv_sem.at[t + 1, uly],
            device_id=(section + 1, p),
            device_id_type=MESH,
        )

    def tick_arrival(t, p):
        return pltpu.make_async_remote_copy(
            src_ref=sent.at[t],
            dst_ref=stream.at[t, p],
            send_sem=tick_send_sem.at[t, 0],
            recv_sem=tick_recv_sem.at[t, p],
            device_id=(section, uly),
            device_id_type=MESH,
        )

    def last_copy(i):
        return pltpu.make_async_remote_copy(
            src_ref=last_send.at[peers[i]],
            dst_ref=last_recv.at[uly],
            send_sem=last_send_sem.at[i],
            recv_sem=last_recv_sem.at[uly],
            device_id=(section, peers[i]),
            device_id_type=MESH,
        )

    def last_arrival(p):
        return pltpu.make_async_remote_copy(
            src_ref=last_send.at[p],
            dst_ref=last_recv.at[p],
            send_sem=last_send_sem.at[0],
            recv_sem=last_recv_sem.at[p],
            device_id=(section, p),
            device_id_type=MESH,
        )

    own_gate = gate[:, pl.ds(pl.multiple_of(uly * local, local), local)]
    for t in range(ticks):

        @pl.when(section == 0)
        def _():
            rows_to_stream(t)

        if t == 0:

            @pl.when(section > 0)
            def _():
                rows_to_stream(t)

        def arrived(c):
            if t > 0:

                @pl.when(section > 0)
                def _():
                    tick_arrival(t, c).wait_recv()

        queries, new_keys, new_values = project(
            stream.at[t], nearest_first, arrived, w, plain_sum, shift_sum, local, width
        )
        new_keys = new_keys.astype(BF16)
        new_values = new_values.astype(BF16)
        at = pl.ds(t * pr, pr)
        keys_met[at, :] = normed(new_keys.astype(F32), k_row, hd).astype(BF16)
        values_met[at, :] = new_values
        new[0, at, :] = new_keys
        new[1, at, :] = new_values
        attended = attend(
            queries, q_row, keys_kept, values_kept, keys_met, values_met, valid, hd
        )
        result = stream[t, uly].astype(F32) + own_gate * attended.astype(BF16).astype(F32)

        if t < ticks - 1:
            sent[t] = result.astype(BF16)

            @pl.when(section < sections - 1)
            def _():
                for i, p in enumerate([*peers, uly]):
                    tick_copy(t, i, p).start()
        else:
            for i in range(group):
                piece = result[i * rows_dev : (i + 1) * rows_dev]
                last_send[i] = jnp.concatenate(
                    [piece[:, c * hd : (c + 1) * hd] for c in range(heads)], axis=0
                ).astype(BF16)
            for i in range(group - 1):
                last_copy(i).start()
            last_recv[uly] = last_send[uly]

    for b in range(patches):
        for i in range(2):
            rows = image[i, pl.ds(b * pr, pr), :]
            for j in range(ticks):
                rows = jnp.where(patch_at(j) == b, new[i, pl.ds(j * pr, pr), :], rows)
            cache_out[i, pl.ds(b * pr, pr), :] = rows
    for i in range(group - 1):
        row_copy(0, i).wait_send()

    @pl.when(section == 0)
    def _():
        for t in range(1, ticks):
            for i in range(group - 1):
                row_copy(t, i).wait_send()

    @pl.when(section < sections - 1)
    def _():
        for t in range(ticks - 1):
            for i, p in enumerate([*peers, uly]):
                tick_copy(t, i, p).wait_send()

    for i in range(group - 1):
        last_copy(i).wait_send()
    for p in peers:
        last_arrival(p).wait_recv()
    for i in range(group):
        piece = last_recv[i].astype(F32)
        for c in range(heads):
            out[:, pl.ds(i * local + c * hd, hd)] = piece[
                c * rows_dev : (c + 1) * rows_dev
            ].astype(BF16)


def store_kernel(rows, cache, out_hbm, cache_hbm, sems):
    copies = [
        pltpu.make_async_copy(src, dst, sems.at[i])
        for i, (src, dst) in enumerate([(rows, out_hbm), (cache, cache_hbm)])
    ]
    for copy in copies:
        copy.start()
    for copy in copies:
        copy.wait()


def in_hbm(*arrays):
    return [pltpu.with_memory_space_constraint(array, pltpu.HBM) for array in arrays]


def in_vmem(*arrays):
    return [pltpu.with_memory_space_constraint(array, pltpu.VMEM) for array in arrays]


def body(
    block_in,
    fresh_patches,
    w_qkv,
    mod_shift,
    mod_scale,
    gate,
    q_gain,
    k_gain,
    image_cache,
    text_cache,
    patch_order,
    text_length,
):
    sections, group = lax.axis_size("section"), lax.axis_size("uly")
    rows_dev, width = block_in.shape[1:]
    local = w_qkv.shape[3]
    hd = q_gain.shape[1]
    patches = patch_order.shape[0]
    ticks = fresh_patches.shape[0] + 1
    pr = rows_dev * group
    txt = text_cache.shape[2]
    img = patches * pr
    heads = local // hd
    kept = txt + (patches - ticks) * pr
    dims = (sections, group, ticks, patches, pr, width, local, hd, txt)
    hbm = pl.BlockSpec(memory_space=pl.ANY)
    dma = pltpu.SemaphoreType.DMA
    vmem = pltpu.VMEM
    rows, cache = pl.pallas_call(
        functools.partial(relay_kernel, dims),
        out_shape=(
            jax.ShapeDtypeStruct((rows_dev, width), BF16),
            jax.ShapeDtypeStruct((2, img, local), BF16),
        ),
        in_specs=[hbm] * 12,
        out_specs=(pl.BlockSpec(memory_space=pltpu.VMEM),) * 2,
        scratch_shapes=[
            vmem((rows_dev, width), BF16),
            vmem((ticks - 1, rows_dev, width), BF16),
            vmem((3, width, local), BF16),
            vmem((1, width), F32),
            vmem((1, width), F32),
            vmem((1, width), F32),
            vmem((1, hd), F32),
            vmem((1, hd), F32),
            vmem((2, img, local), BF16),
            vmem((2, txt, local), BF16),
            pltpu.SMEM((patches,), jnp.int32),
            pltpu.SMEM((1,), jnp.int32),
            vmem((3, 1, local), F32),
            vmem((3, 1, local), F32),
            vmem((kept, local), BF16),
            vmem((kept, local), BF16),
            vmem((ticks * pr, local), BF16),
            vmem((ticks * pr, local), BF16),
            vmem((2, ticks * pr, local), BF16),
            vmem((ticks, group, pr, local), BF16),
            vmem((ticks, pr, local), BF16),
            vmem((ticks, 2 * rows_dev, width // 2), BF16),
            vmem((ticks, group, 2 * rows_dev, width // 2), BF16),
            vmem((group, heads * rows_dev, hd), BF16),
            vmem((group, heads * rows_dev, hd), BF16),
            dma((12,)),
            dma((ticks, group)),
            dma((ticks, group)),
            dma((ticks, group)),
            dma((ticks, group)),
            dma((group,)),
            dma((group,)),
        ],
        compiler_params=pltpu.CompilerParams(
            collective_id=0, has_side_effects=True, vmem_limit_bytes=VMEM_LIMIT
        ),
        name="relay",
    )(
        *in_hbm(
            block_in[0],
            fresh_patches,
            jnp.transpose(w_qkv[0], (1, 0, 2)),
            mod_shift,
            mod_scale,
            gate,
            q_gain,
            k_gain,
            image_cache[0],
            text_cache[0],
            patch_order,
        ),
        text_length,
    )
    out, cache = pl.pallas_call(
        store_kernel,
        out_shape=(
            jax.ShapeDtypeStruct((rows_dev, width), BF16),
            jax.ShapeDtypeStruct((2, img, local), BF16),
        ),
        in_specs=[hbm] * 2,
        out_specs=(hbm, hbm),
        scratch_shapes=[dma((2,))],
        compiler_params=pltpu.CompilerParams(vmem_limit_bytes=VMEM_LIMIT),
        name="outputs",
    )(*in_vmem(rows, cache))
    return out[None], cache[None]


def solution(mesh):
    in_specs = (
        P("section", "uly", None),
        P(None, "uly", None),
        P("section", None, None, "uly"),
        P("section", None),
        P("section", None),
        P("section", None),
        P("section", None),
        P("section", None),
        P("section", None, None, "uly"),
        P("section", None, None, "uly"),
        P(),
        P(),
    )
    out_specs = (P("section", "uly", None), P("section", None, None, "uly"))
    return jax.shard_map(body, mesh=mesh, in_specs=in_specs, out_specs=out_specs, check_vma=False)
```

```python
import functools
import math

import jax
import jax.numpy as jnp
from jax import lax
from jax.experimental import pallas as pl
from jax.experimental.pallas import tpu as pltpu
from jax.sharding import PartitionSpec as P

MESH = pl.DeviceIdType.MESH
F32 = jnp.float32
BF16 = jnp.bfloat16
EPS = 1e-06
VMEM_LIMIT = 48 * 1024 * 1024


def head_factor(values):
    return lax.rsqrt(jnp.mean(values * values, axis=-1, keepdims=True) + EPS)


def normed(values, gain, head_dim):
    parts = []
    for start in range(0, values.shape[1], head_dim):
        part = values[:, start : start + head_dim]
        parts.append(part * head_factor(part) * gain)
    return jnp.concatenate(parts, axis=1)


def fold(w, shift, scale, plain_sum, shift_sum, local, start, stop):
    block = 256
    first = lax.broadcasted_iota(jnp.int32, (16, block), 0)
    ones = jnp.ones((16, block), BF16)

    def step(i, totals):
        at = pl.ds(pl.multiple_of(i * block, block), block)
        shift_row = shift[:, at]
        high = shift_row.astype(BF16).astype(F32)
        both = jnp.where(first == 0, high, jnp.where(first == 1, shift_row - high, 0.0))
        both = both.astype(BF16)
        factors = []
        for part in range(block // 128):
            row = scale[:, pl.ds(pl.multiple_of(i * block + part * 128, 128), 128)]
            factors.append(jnp.transpose(jnp.broadcast_to(1.0 + row, (128, 128))))
        factor = jnp.concatenate(factors, axis=0)
        new = []
        for j in range(3):
            rows = w[j, at, :]
            folded = jnp.concatenate(
                [
                    (rows[:, c : c + 128].astype(F32) * factor).astype(BF16)
                    for c in range(0, local, 128)
                ],
                axis=1,
            )
            w[j, at, :] = folded
            new.append(totals[2 * j] + jnp.dot(ones, folded, preferred_element_type=F32))
            new.append(totals[2 * j + 1] + jnp.dot(both, rows, preferred_element_type=F32))
        return tuple(new)

    zero = jnp.zeros((16, local), F32)
    totals = lax.fori_loop(start, stop, step, (zero,) * 6)
    for j in range(3):
        plain_sum[j] += totals[2 * j][:1]
        shift_sum[j] += totals[2 * j + 1][:1] + totals[2 * j + 1][1:2]


def lanes_summed(values):
    return sum(values[:, c : c + 128] for c in range(0, values.shape[1], 128))


def project(stream, order, arrived, w, plain_sum, shift_sum, local, width):
    near = len(order) // 2
    sums = [None] * 3

    def add(chunk, c):
        at = pl.ds(pl.multiple_of(c * local, local), local)
        for j in range(3):
            product = jnp.dot(chunk, w[j, at, :], preferred_element_type=F32)
            sums[j] = product if sums[j] is None else sums[j] + product

    values = []
    for c in order[:near]:
        arrived(c)
        chunk = stream[c]
        add(chunk, c)
        values.append(chunk.astype(F32))
    pivot = jnp.sum(lanes_summed(sum(values)), axis=-1, keepdims=True) / (near * local)
    off = [value - pivot for value in values]
    first = lanes_summed(sum(off))
    second = lanes_summed(sum(o * o for o in off))
    for c in order[near:]:
        arrived(c)
        chunk = stream[c]
        add(chunk, c)
        o = chunk.astype(F32) - pivot
        first = first + lanes_summed(o)
        second = second + lanes_summed(o * o)
    beyond = jnp.sum(first, axis=-1, keepdims=True) / width
    variance = jnp.sum(second, axis=-1, keepdims=True) / width - beyond * beyond
    factor = lax.rsqrt(variance + EPS)
    mean = pivot + beyond
    return [factor * (sums[j] - mean * plain_sum[j]) + shift_sum[j] for j in range(3)]


def attend(queries, q_row, keys_kept, values_kept, keys_met, values_met, valid, hd):
    rows, txt = queries.shape[0], valid.shape[1]
    heads = queries.shape[1] // hd
    stacked, factors = [], []
    for h in range(heads):
        query = queries[:, h * hd : (h + 1) * hd]
        factors.append(head_factor(query) * (1.0 / math.sqrt(hd)))
        parts = [jnp.zeros((rows, hd), BF16)] * heads
        parts[h] = (query * q_row).astype(BF16)
        stacked.append(jnp.concatenate(parts, axis=1))
    stacked = jnp.concatenate(stacked, axis=0)
    factor = jnp.concatenate(factors, axis=0)
    contract = (((1,), (1,)), ((), ()))
    kept = lax.dot_general(stacked, keys_kept[...], contract, preferred_element_type=F32)
    met = lax.dot_general(stacked, keys_met[...], contract, preferred_element_type=F32)
    kept = jnp.exp(kept * factor)
    met = jnp.exp(met * factor)
    kept = jnp.concatenate([kept[:, :txt] * valid, kept[:, txt:]], axis=1)
    total = jnp.sum(lanes_summed(kept) + lanes_summed(met), axis=-1, keepdims=True)
    mixed = jnp.dot(
        kept.astype(BF16), values_kept[...], preferred_element_type=F32
    ) + jnp.dot(met.astype(BF16), values_met[...], preferred_element_type=F32)
    mixed = mixed / total
    return jnp.concatenate(
        [mixed[h * rows : (h + 1) * rows, h * hd : (h + 1) * hd] for h in range(heads)], axis=1
    )


def relay_kernel(
    dims,
    block_hbm,
    fresh_hbm,
    w_hbm,
    shift_hbm,
    scale_hbm,
    gate_hbm,
    q_gain_hbm,
    k_gain_hbm,
    image_hbm,
    text_hbm,
    order_hbm,
    length_hbm,
    out,
    cache_out,
    block,
    fresh,
    w,
    shift,
    scale,
    gate,
    q_gain,
    k_gain,
    image,
    text,
    order,
    length,
    plain_sum,
    shift_sum,
    keys_kept,
    values_kept,
    keys_met,
    values_met,
    new,
    stream,
    sent,
    row_send,
    row_recv,
    last_send,
    last_recv,
    load_sem,
    row_send_sem,
    row_recv_sem,
    tick_send_sem,
    tick_recv_sem,
    last_send_sem,
    last_recv_sem,
):
    sections, group, ticks, patches, pr, width, local, hd, txt = dims
    heads = local // hd
    rows_dev = pr // group
    half = width // 2
    section = lax.axis_index("section")
    uly = lax.axis_index("uly")

    other = uly + 1 - 2 * lax.rem(uly, 2)
    across = [lax.rem(other + k, group) for k in (4, 2, 6, 0)]
    beside = [lax.rem(uly + k, group) for k in (4, 2, 6)]
    peers = across + beside
    nearest_first = [uly, *beside[1:], beside[0], across[3], across[1], across[2], across[0]]

    barrier = pltpu.get_barrier_semaphore()
    for p in peers:
        pl.semaphore_signal(barrier, inc=1, device_id=(section, p), device_id_type=MESH)

    @pl.when(section > 0)
    def _():
        for p in [*peers, uly]:
            pl.semaphore_signal(barrier, inc=1, device_id=(section - 1, p), device_id_type=MESH)

    loads = [
        pltpu.make_async_copy(src, dst, load_sem.at[i])
        for i, (src, dst) in enumerate(
            [
                (block_hbm, block),
                (fresh_hbm, fresh),
                (text_hbm, text),
                (k_gain_hbm, k_gain),
                (image_hbm, image),
                (order_hbm, order),
                (length_hbm, length),
                (shift_hbm, shift),
                (scale_hbm, scale),
                (gate_hbm, gate),
                (q_gain_hbm, q_gain),
                (w_hbm, w),
            ]
        )
    ]
    for copy in loads:
        copy.start()

    loads[0].wait()
    loads[1].wait()
    for t in range(ticks):
        own = block[...] if t == 0 else fresh[t - 1]
        own = own.astype(F32)
        own = jnp.concatenate([own[:, :half], own[:, half:]], axis=0).astype(BF16)
        row_send[t] = own
        row_recv[t, uly] = own

    def patch_at(slot):
        return order[lax.rem(slot - section + sections * patches, patches)]

    for copy in loads[2:7]:
        copy.wait()
    k_row = k_gain[...]
    keys_kept[pl.ds(0, txt), :] = normed(text[0].astype(F32), k_row, hd).astype(BF16)
    values_kept[pl.ds(0, txt), :] = text[1]
    for j in range(patches):
        patch = patch_at(j)
        met = []
        for i in range(2):
            rows = image[i, pl.ds(0, pr), :]
            for b in range(1, patches):
                rows = jnp.where(patch == b, image[i, pl.ds(b * pr, pr), :], rows)
            met.append(rows)
        keys, values, at = (
            (keys_met, values_met, pl.ds(j * pr, pr))
            if j < ticks
            else (keys_kept, values_kept, pl.ds(txt + (j - ticks) * pr, pr))
        )
        keys[at, :] = normed(met[0].astype(F32), k_row, hd).astype(BF16)
        values[at, :] = met[1]
    valid = (lax.broadcasted_iota(jnp.int32, (1, txt), 1) < length[0]).astype(F32)

    pl.semaphore_wait(barrier, group - 1 + jnp.where(section < sections - 1, group, 0))

    def row_copy(t, i):
        return pltpu.make_async_remote_copy(
            src_ref=row_send.at[t],
            dst_ref=row_recv.at[t, uly],
            send_sem=row_send_sem.at[t, i],
            recv_sem=row_recv_sem.at[t, uly],
            device_id=(section, peers[i]),
            device_id_type=MESH,
        )

    def row_arrival(t, p):
        return pltpu.make_async_remote_copy(
            src_ref=row_send.at[t],
            dst_ref=row_recv.at[t, p],
            send_sem=row_send_sem.at[t, 0],
            recv_sem=row_recv_sem.at[t, p],
            device_id=(section, p),
            device_id_type=MESH,
        )

    for copy in loads[7:]:
        copy.wait()
    q_row = q_gain[...]
    plain_sum[...] = jnp.zeros_like(plain_sum)
    shift_sum[...] = jnp.zeros_like(shift_sum)
    blocks = width // 256
    ahead = jnp.where(lax.rem(section, 2) == 0, blocks * 3 // 4, 0)
    fold(w, shift, scale, plain_sum, shift_sum, local, 0, ahead)

    for i in range(group - 1):
        row_copy(0, i).start()

    @pl.when(section == 0)
    def _():
        for t in range(1, ticks):
            for i in range(group - 1):
                row_copy(t, i).start()

    fold(w, shift, scale, plain_sum, shift_sum, local, ahead, blocks)

    def rows_to_stream(t):
        for p in peers:
            row_arrival(t, p).wait_recv()
        pieces = [row_recv[t, i].astype(F32) for i in range(group)]
        for side in range(2):
            whole = jnp.concatenate(
                [piece[side * rows_dev : (side + 1) * rows_dev] for piece in pieces], axis=0
            ).astype(BF16)
            for c in range(group // 2):
                stream[t, side * (group // 2) + c] = whole[:, c * local : (c + 1) * local]

    def tick_copy(t, i, p):
        return pltpu.make_async_remote_copy(
            src_ref=sent.at[t],
            dst_ref=stream.at[t + 1, uly],
            send_sem=tick_send_sem.at[t, i],
            recv_sem=tick_recv_sem.at[t + 1, uly],
            device_id=(section + 1, p),
            device_id_type=MESH,
        )

    def tick_arrival(t, p):
        return pltpu.make_async_remote_copy(
            src_ref=sent.at[t],
            dst_ref=stream.at[t, p],
            send_sem=tick_send_sem.at[t, 0],
            recv_sem=tick_recv_sem.at[t, p],
            device_id=(section, uly),
            device_id_type=MESH,
        )

    def last_copy(i):
        return pltpu.make_async_remote_copy(
            src_ref=last_send.at[peers[i]],
            dst_ref=last_recv.at[uly],
            send_sem=last_send_sem.at[i],
            recv_sem=last_recv_sem.at[uly],
            device_id=(section, peers[i]),
            device_id_type=MESH,
        )

    def last_arrival(p):
        return pltpu.make_async_remote_copy(
            src_ref=last_send.at[p],
            dst_ref=last_recv.at[p],
            send_sem=last_send_sem.at[0],
            recv_sem=last_recv_sem.at[p],
            device_id=(section, p),
            device_id_type=MESH,
        )

    own_gate = gate[:, pl.ds(pl.multiple_of(uly * local, local), local)]
    for t in range(ticks):

        @pl.when(section == 0)
        def _():
            rows_to_stream(t)

        if t == 0:

            @pl.when(section > 0)
            def _():
                rows_to_stream(t)

        def arrived(c):
            if t > 0:

                @pl.when(section > 0)
                def _():
                    tick_arrival(t, c).wait_recv()

        queries, new_keys, new_values = project(
            stream.at[t], nearest_first, arrived, w, plain_sum, shift_sum, local, width
        )
        new_keys = new_keys.astype(BF16)
        new_values = new_values.astype(BF16)
        at = pl.ds(t * pr, pr)
        keys_met[at, :] = normed(new_keys.astype(F32), k_row, hd).astype(BF16)
        values_met[at, :] = new_values
        new[0, at, :] = new_keys
        new[1, at, :] = new_values
        attended = attend(
            queries, q_row, keys_kept, values_kept, keys_met, values_met, valid, hd
        )
        result = stream[t, uly].astype(F32) + own_gate * attended.astype(BF16).astype(F32)

        if t < ticks - 1:
            sent[t] = result.astype(BF16)

            @pl.when(section < sections - 1)
            def _():
                for i, p in enumerate([*peers, uly]):
                    tick_copy(t, i, p).start()
        else:
            for i in range(group):
                piece = result[i * rows_dev : (i + 1) * rows_dev]
                last_send[i] = jnp.concatenate(
                    [piece[:, c * hd : (c + 1) * hd] for c in range(heads)], axis=0
                ).astype(BF16)
            for i in range(group - 1):
                last_copy(i).start()
            last_recv[uly] = last_send[uly]

    for b in range(patches):
        for i in range(2):
            rows = image[i, pl.ds(b * pr, pr), :]
            for j in range(ticks):
                rows = jnp.where(patch_at(j) == b, new[i, pl.ds(j * pr, pr), :], rows)
            cache_out[i, pl.ds(b * pr, pr), :] = rows
    for i in range(group - 1):
        row_copy(0, i).wait_send()

    @pl.when(section == 0)
    def _():
        for t in range(1, ticks):
            for i in range(group - 1):
                row_copy(t, i).wait_send()

    @pl.when(section < sections - 1)
    def _():
        for t in range(ticks - 1):
            for i, p in enumerate([*peers, uly]):
                tick_copy(t, i, p).wait_send()

    for i in range(group - 1):
        last_copy(i).wait_send()
    for p in peers:
        last_arrival(p).wait_recv()
    for i in range(group):
        piece = last_recv[i].astype(F32)
        for c in range(heads):
            out[:, pl.ds(i * local + c * hd, hd)] = piece[
                c * rows_dev : (c + 1) * rows_dev
            ].astype(BF16)


def store_kernel(rows, cache, out_hbm, cache_hbm, sems):
    copies = [
        pltpu.make_async_copy(src, dst, sems.at[i])
        for i, (src, dst) in enumerate([(rows, out_hbm), (cache, cache_hbm)])
    ]
    for copy in copies:
        copy.start()
    for copy in copies:
        copy.wait()


def in_hbm(*arrays):
    return [pltpu.with_memory_space_constraint(array, pltpu.HBM) for array in arrays]


def in_vmem(*arrays):
    return [pltpu.with_memory_space_constraint(array, pltpu.VMEM) for array in arrays]


def body(
    block_in,
    fresh_patches,
    w_qkv,
    mod_shift,
    mod_scale,
    gate,
    q_gain,
    k_gain,
    image_cache,
    text_cache,
    patch_order,
    text_length,
):
    sections, group = lax.axis_size("section"), lax.axis_size("uly")
    rows_dev, width = block_in.shape[1:]
    local = w_qkv.shape[3]
    hd = q_gain.shape[1]
    patches = patch_order.shape[0]
    ticks = fresh_patches.shape[0] + 1
    pr = rows_dev * group
    txt = text_cache.shape[2]
    img = patches * pr
    heads = local // hd
    kept = txt + (patches - ticks) * pr
    dims = (sections, group, ticks, patches, pr, width, local, hd, txt)
    hbm = pl.BlockSpec(memory_space=pl.ANY)
    dma = pltpu.SemaphoreType.DMA
    vmem = pltpu.VMEM
    rows, cache = pl.pallas_call(
        functools.partial(relay_kernel, dims),
        out_shape=(
            jax.ShapeDtypeStruct((rows_dev, width), BF16),
            jax.ShapeDtypeStruct((2, img, local), BF16),
        ),
        in_specs=[hbm] * 12,
        out_specs=(pl.BlockSpec(memory_space=pltpu.VMEM),) * 2,
        scratch_shapes=[
            vmem((rows_dev, width), BF16),
            vmem((ticks - 1, rows_dev, width), BF16),
            vmem((3, width, local), BF16),
            vmem((1, width), F32),
            vmem((1, width), F32),
            vmem((1, width), F32),
            vmem((1, hd), F32),
            vmem((1, hd), F32),
            vmem((2, img, local), BF16),
            vmem((2, txt, local), BF16),
            pltpu.SMEM((patches,), jnp.int32),
            pltpu.SMEM((1,), jnp.int32),
            vmem((3, 1, local), F32),
            vmem((3, 1, local), F32),
            vmem((kept, local), BF16),
            vmem((kept, local), BF16),
            vmem((ticks * pr, local), BF16),
            vmem((ticks * pr, local), BF16),
            vmem((2, ticks * pr, local), BF16),
            vmem((ticks, group, pr, local), BF16),
            vmem((ticks, pr, local), BF16),
            vmem((ticks, 2 * rows_dev, width // 2), BF16),
            vmem((ticks, group, 2 * rows_dev, width // 2), BF16),
            vmem((group, heads * rows_dev, hd), BF16),
            vmem((group, heads * rows_dev, hd), BF16),
            dma((12,)),
            dma((ticks, group)),
            dma((ticks, group)),
            dma((ticks, group)),
            dma((ticks, group)),
            dma((group,)),
            dma((group,)),
        ],
        compiler_params=pltpu.CompilerParams(
            collective_id=0, has_side_effects=True, vmem_limit_bytes=VMEM_LIMIT
        ),
        name="relay",
    )(
        *in_hbm(
            block_in[0],
            fresh_patches,
            jnp.transpose(w_qkv[0], (1, 0, 2)),
            mod_shift,
            mod_scale,
            gate,
            q_gain,
            k_gain,
            image_cache[0],
            text_cache[0],
            patch_order,
        ),
        text_length,
    )
    out, cache = pl.pallas_call(
        store_kernel,
        out_shape=(
            jax.ShapeDtypeStruct((rows_dev, width), BF16),
            jax.ShapeDtypeStruct((2, img, local), BF16),
        ),
        in_specs=[hbm] * 2,
        out_specs=(hbm, hbm),
        scratch_shapes=[dma((2,))],
        compiler_params=pltpu.CompilerParams(vmem_limit_bytes=VMEM_LIMIT),
        name="outputs",
    )(*in_vmem(rows, cache))
    return out[None], cache[None]


def solution(mesh):
    in_specs = (
        P("section", "uly", None),
        P(None, "uly", None),
        P("section", None, None, "uly"),
        P("section", None),
        P("section", None),
        P("section", None),
        P("section", None),
        P("section", None),
        P("section", None, None, "uly"),
        P("section", None, None, "uly"),
        P(),
        P(),
    )
    out_specs = (P("section", "uly", None), P("section", None, None, "uly"))
    return jax.shard_map(body, mesh=mesh, in_specs=in_specs, out_specs=out_specs, check_vma=False)
```
